256 devices in a mesh: blk: 128 (over z, x, y_lo, core), seg: 2 (over y_hi).
Axes of the slice: x: 4, y: 4 (y_hi: 2, y_lo: 2; y = y_hi * 2 + y_lo), z: 8, core: 2. Of those that a mesh axis runs over, the one named last changes fastest.
Arguments:
- records: float32 [128, 60, 3, 3000], P('blk', 'seg')
- availability: int32 [128, 60], P('blk', 'seg'), may hold values from 0 to 1, as said below
Outputs:
- correlations: bfloat16 [128, 128, 9, 2048], P('blk', 'seg')
The draws below stay inside these ranges and needn't reach their ends.
Inputs may be any that keep to these rules, and one draw needn't show every extreme that they name: `availability`: every station has at least one recorded segment.
All inputs are finite; a program needn't handle non-finite values.
Results may differ from the reference program's by a relative error of at most 0.0053.
Values may be sent and summed in bfloat16 or wider, within the bound.
A program may use at most 128 MiB of HBM per device.

```python
import jax
import jax.numpy as jnp
from jax import lax

SEGS = 60
SAMPLES = 3000
NFFT = 4096
FREQS = 512
WIDTH = 32
LAG = 1024
STATIONS = 128


def draw_records(key, part):
    key = jax.random.fold_in(key, 11)
    noise_key, level_key = jax.random.split(key)
    shape = (STATIONS, SEGS, 3, SAMPLES)
    noise = jax.random.normal(noise_key, shape, jnp.float32)
    level = jax.random.uniform(level_key, (STATIONS, SEGS, 3, 1), jnp.float32, -1.2, 1.2)
    return noise * jnp.exp(level)


def draw_availability(key, part):
    key = jax.random.fold_in(key, 23)
    rate_key, pick_key, anchor_key = jax.random.split(key, 3)
    rate = jax.random.randint(rate_key, (STATIONS, 1), 2, 10)
    pick = jax.random.randint(pick_key, (STATIONS, SEGS), 0, 10)
    anchor = jax.random.randint(anchor_key, (STATIONS, 1), 0, SEGS)
    column = lax.iota(jnp.int32, SEGS)[None, :]
    return jnp.where((pick < rate) | (column == anchor), 1, 0).astype(jnp.int32)


def setup_inputs(seed: int = 0) -> dict:
    arg_keys = jax.random.split(jax.random.key(seed), 3)
    return {
        "records": draw_records(jax.random.fold_in(arg_keys[2], 71), 0),
        "availability": draw_availability(jax.random.fold_in(arg_keys[2], 71), 0),
    }


def reference(records, availability):
    spec = jnp.fft.rfft(records, n=NFFT, axis=-1)[..., 1:FREQS + 1]
    spectra = jnp.concatenate([jnp.real(spec), jnp.imag(spec)], axis=-1).astype(jnp.float32)
    power = spectra[..., :FREQS] ** 2 + spectra[..., FREQS:] ** 2
    power = power.reshape(STATIONS, SEGS, 3, FREQS // WIDTH, WIDTH)
    amplitude = jnp.sqrt(lax.optimization_barrier(jnp.mean(power, axis=(2, 4))) + 1e-06)
    amplitude = jnp.repeat(amplitude, WIDTH, axis=2)
    present = availability.astype(jnp.float32)
    totals = lax.optimization_barrier(jnp.sum(present, axis=1))
    weight = present / jnp.sqrt(totals)[:, None]
    factor = weight[:, :, None] / amplitude
    factor = jnp.concatenate([factor, factor], axis=-1)[:, :, None, :]
    white = (spectra * factor).astype(jnp.bfloat16)
    white_re = white[..., :FREQS].astype(jnp.float32)
    white_im = white[..., FREQS:].astype(jnp.float32)

    def one_row(index):
        own_re = lax.dynamic_slice_in_dim(white_re, index, 1, 0)
        own_im = lax.dynamic_slice_in_dim(white_im, index, 1, 0)
        real = jnp.einsum('isak,jsbk->iajbk', own_re, white_re) + jnp.einsum('isak,jsbk->iajbk', own_im, white_im)
        imag = jnp.einsum('isak,jsbk->iajbk', own_im, white_re) - jnp.einsum('isak,jsbk->iajbk', own_re, white_im)
        spectrum = lax.complex(real, imag)[0]
        spectrum = jnp.transpose(spectrum, (1, 0, 2, 3)).reshape(STATIONS, 9, FREQS)
        full = jnp.zeros((STATIONS, 9, NFFT // 2 + 1), spectrum.dtype).at[..., 1:FREQS + 1].set(spectrum)
        wave = jnp.fft.irfft(full, n=NFFT, axis=-1)
        return jnp.concatenate([wave[..., NFFT - LAG:], wave[..., :LAG]], axis=-1).astype(jnp.bfloat16)
    return lax.map(one_row, jnp.arange(STATIONS, dtype=jnp.int32))
```

```python
import functools
import math

import jax
import jax.numpy as jnp
import ml_dtypes
import numpy as np
from jax import lax
from jax.experimental import pallas as pl
from jax.experimental.pallas import tpu as pltpu
from jax.sharding import PartitionSpec as P

MESH = pl.DeviceIdType.MESH
F32 = jnp.float32
BF16 = jnp.bfloat16
NFFT = 4096
FREQS = 512
LAG = 1024
SEGS = 30
ROWS = 96
RESIDUES = ((1, 7), (2, 6), (3, 5), (8, 4))
HALF = math.sqrt(0.5)
NT = (((1,), (1,)), ((), ()))


def bin_of(p, f):
    return 16 * p + 8 * (f % 2) + np.array(RESIDUES)[f // 4, f // 2 % 2]


def forward_table():
    table = np.zeros((4, 32, 2, 2, 2, 2, 512))
    n = np.arange(512)
    for g in range(4):
        for which in range(2):
            for odd in range(2):
                k = 16 * np.arange(32) + 8 * odd + RESIDUES[g][which]
                angle = (k[:, None] * n[None, :] % NFFT) * (2 * np.pi / NFFT)
                cos, sin = np.cos(angle), np.sin(angle)
                if g == 3:
                    table[g, :, which, odd, 0, which] = cos
                    table[g, :, which, odd, 1, which] = -sin
                else:
                    sign = 1 - 2 * which
                    table[g, :, which, odd, 0, 0] = cos
                    table[g, :, which, odd, 0, 1] = sign * sin
                    table[g, :, which, odd, 1, 0] = -sin
                    table[g, :, which, odd, 1, 1] = sign * cos
    table = table.reshape(4, 256, 1024)
    high = table.astype(ml_dtypes.bfloat16)
    low = (table - high.astype(np.float64)).astype(ml_dtypes.bfloat16)
    return high, low


def inverse_table():
    p, f = np.meshgrid(np.arange(32), np.arange(16), indexing="ij")
    k = bin_of(p, f).reshape(-1)
    tau = np.arange(2 * LAG) - LAG
    angle = (k[:, None] * tau[None, :] % NFFT) * (2 * np.pi / NFFT)
    table = np.concatenate([np.cos(angle), -np.sin(angle)], axis=0) * (2.0 / NFFT)
    return table.astype(ml_dtypes.bfloat16)


def place_table():
    plain = np.zeros((2, 2, 128, 3, 128))
    turned = np.zeros((2, 2, 128, 3, 128))
    for seg in range(2):
        for s in range(SEGS):
            for c in range(3):
                for part in range(2):
                    plain[seg, part, 3 * s + c, c, 64 * part + 30 * seg + s] = 1
                turned[seg, 1, 3 * s + c, c, 30 * seg + s] = 1
                turned[seg, 0, 3 * s + c, c, 64 + 30 * seg + s] = -1
    both = np.stack([plain, turned]).reshape(2, 512, 384)
    return both.astype(ml_dtypes.bfloat16)


def place():
    blk, seg = lax.axis_index("blk"), lax.axis_index("seg")
    z, rest = blk // 16, blk % 16
    return z, rest // 4, seg * 2 + rest // 2 % 2, rest % 2, seg


def device(z, x, y, core):
    return (z * 16 + x * 4 + y % 2 * 2 + core, y // 2)


def partner(t, x, y, core):
    return (x + 2 + t // 8) % 4, (y + 2 + t // 2 % 4) % 4, (core + 1 + t) % 2


def spread(av):
    column = lax.broadcasted_iota(jnp.int32, (SEGS, 128), 1)
    row = lax.broadcasted_iota(jnp.int32, (SEGS, 128), 0)
    pick = ((column >= 3 * row) & (column < 3 * row + 3)).astype(F32)
    return jnp.dot(jnp.broadcast_to(av, (8, SEGS)), pick, preferred_element_type=F32)


def split_rows(w_ref, g, half, value):
    high = value.astype(BF16)
    low = (value - high.astype(F32)).astype(BF16)
    columns = pl.ds(512 * half, 512)
    w_ref[g, pl.ds(0, ROWS), columns] = high
    w_ref[g, pl.ds(128, ROWS), columns] = low


def stack_kernel(
    x_ref, av_ref, high_ref, low_ref, place_ref, out_ref,
    w, xs, white, rin, turn, gathered, left, stage, send, counts,
    count_sem, in_sem, ring_send, ring_recv, out_sem, own_sem,
):
    z, x, y, core, seg = place()
    slot = (x * 4 + y % 2 * 2 + core) * 2 + seg
    up, down = (z + 1) % 8, (z + 7) % 8
    barrier = pltpu.get_barrier_semaphore()

    def greet(t, carry):
        px, py, pc = partner(t, x, y, core)
        pl.semaphore_signal(barrier, inc=1, device_id=device(z, px, py, pc), device_id_type=MESH)
        return carry

    lax.fori_loop(0, 21, greet, 0)
    lax.fori_loop(22, 32, greet, 0)
    for other in (up, down):
        pl.semaphore_signal(barrier, inc=1, device_id=device(other, x, y, core), device_id_type=MESH)

    own = spread(av_ref[...].astype(F32))
    counts[0] = own
    part = [x_ref[:, 512 * n : 512 * (n + 1)] for n in range(6)]
    for g in range(4):
        for start in (ROWS, 128 + ROWS):
            w[g, pl.ds(start, 32), :] = jnp.zeros((32, 1024), BF16)
    d04 = part[0] - part[4]
    d13, s13 = part[1] - part[3], part[1] + part[3]
    split_rows(w, 0, 0, d04 + (d13 - part[5]) * HALF)
    split_rows(w, 0, 1, (part[5] - s13) * HALF - part[2])
    split_rows(w, 1, 0, part[0] + part[4] - part[2])
    split_rows(w, 1, 1, part[3] - part[1] - part[5])
    split_rows(w, 2, 0, d04 + (part[5] - d13) * HALF)
    split_rows(w, 2, 1, (part[5] - s13) * HALF + part[2])
    even, odd = part[0] + part[2] + part[4], s13 + part[5]
    split_rows(w, 3, 0, even + odd)
    split_rows(w, 3, 1, even - odd)

    pl.semaphore_wait(barrier, 33)
    count_copy = pltpu.make_async_remote_copy(
        src_ref=counts.at[0], dst_ref=counts.at[1], send_sem=count_sem.at[0], recv_sem=count_sem.at[1],
        device_id=device(z, x, (y + 2) % 4, core), device_id_type=MESH,
    )
    count_copy.start()

    power = jnp.zeros((32, 8, 128), F32)
    for g in range(4):
        high = lax.dot_general(high_ref[g], w[g], NT, preferred_element_type=F32)
        low = lax.dot_general(low_ref[g], w[g], NT, preferred_element_type=F32)
        both = high + low
        value = (both[:, :128] + both[:, 128:]).reshape(32, 8, 128)
        xs[:, pl.ds(8 * g, 8), :] = value
        power = power + value * value
    power = jnp.sum(power.reshape(16, 16, 128), axis=1)
    triple = power + pltpu.roll(power, 127, 1) + pltpu.roll(power, 126, 1)
    phase = lax.broadcasted_iota(jnp.int32, (16, 128), 1) % 3
    total = jnp.where(phase == 0, triple, jnp.where(phase == 1, pltpu.roll(triple, 1, 1), pltpu.roll(triple, 2, 1)))
    amplitude = jnp.sqrt(total * (1.0 / 96) + 1e-06)
    count_copy.wait()
    count = (jnp.sum(own, axis=1, keepdims=True) + jnp.sum(counts[1], axis=1, keepdims=True)) * (1.0 / 3)
    weight = own / jnp.sqrt(jnp.round(count))
    factor = weight[0:1] / amplitude
    white[...] = (xs[...].reshape(16, 64, 128) * factor[:, None, :]).reshape(32, 32, 128).astype(BF16)

    def scatter(t, carry):
        px, py, pc = partner(t, x, y, core)
        target = (px * 4 + py % 2 * 2 + pc) * 2 + py // 2
        pltpu.make_async_remote_copy(
            src_ref=white.at[target], dst_ref=rin.at[slot], send_sem=in_sem.at[0], recv_sem=in_sem.at[1],
            device_id=device(z, px, py, pc), device_id_type=MESH,
        ).start()
        return carry

    lax.fori_loop(0, 21, scatter, 0)
    lax.fori_loop(22, 32, scatter, 0)
    pltpu.make_async_copy(rin.at[pl.ds(0, 31)], rin.at[pl.ds(0, 31)], in_sem.at[1]).wait()
    rin[slot] = white[slot]

    def swap(source, carry):
        start = source % 2 * 512 + source // 2
        turn[pl.ds(start, 32, stride=16), :] = rin[source].astype(F32)
        return carry

    lax.fori_loop(0, 32, swap, 0)
    pieces = turn[...].reshape(2, 16, 2, 16, 128)
    rows = jnp.concatenate(
        [pieces[s, :, part].reshape(256, 128).astype(BF16) for s in range(2) for part in range(2)], axis=1
    )
    plain = jnp.dot(rows, place_ref[0], preferred_element_type=F32).astype(BF16)
    turned = jnp.dot(rows, place_ref[1], preferred_element_type=F32).astype(BF16)
    for c in range(3):
        one = plain[:, 128 * c : 128 * (c + 1)].reshape(16, 16, 128)
        gathered[c, z] = one
        left[:, pl.ds(16 * c, 16), :] = one
        left[:, pl.ds(48 + 16 * c, 16), :] = turned[:, 128 * c : 128 * (c + 1)].reshape(16, 16, 128)

    def pass_on(c, hop, way, start):
        source = (z + 9 - hop) % 8 if way == 0 else (z + hop - 1) % 8
        copy = pltpu.make_async_remote_copy(
            src_ref=gathered.at[c, source], dst_ref=gathered.at[c, source],
            send_sem=ring_send.at[c, hop - 1, way], recv_sem=ring_recv.at[c, hop - 1, way],
            device_id=device(up if way == 0 else down, x, y, core), device_id_type=MESH,
        )
        if start:
            copy.start()
        return copy

    def last_hop(c, start):
        source = (z + 5 + 6 * core) % 8
        copy = pltpu.make_async_remote_copy(
            src_ref=gathered.at[c, source], dst_ref=gathered.at[c, source],
            send_sem=ring_send.at[c, 3, 0], recv_sem=ring_recv.at[c, 3, 0],
            device_id=device((z + 1 + 6 * core) % 8, x, y, core), device_id_type=MESH,
        )
        if start:
            copy.start()
        return copy

    def arrive(c, hop):
        if hop == 4:
            last_hop(c, False).wait_recv()
        else:
            for way in range(2):
                pass_on(c, hop, way, False).wait_recv()

    def forward(c, hop):
        if hop == 4:
            last_hop(c, True)
        else:
            for way in range(2):
                pass_on(c, hop, way, True)

    lane = lax.broadcasted_iota(jnp.int32, (16, 128), 1) < 64

    def cross(b):
        def one_bin(f, carry):
            right = gathered[b, :, f].reshape(128, 128)
            product = lax.dot_general(left[f], right, NT, preferred_element_type=F32)
            for a in range(3):
                re = product[16 * a : 16 * (a + 1)]
                im = product[48 + 16 * a : 48 + 16 * (a + 1)]
                mixed = pltpu.roll(jnp.where(lane, im, re), 64, 1)
                stage[pl.ds(512 * a + f, 16, stride=16), :] = jnp.where(lane, re, mixed)
                stage[pl.ds(512 * a + 256 + f, 16, stride=16), :] = jnp.where(lane, mixed, im)
            return carry

        lax.fori_loop(0, 16, one_bin, 0)
        send[b] = jnp.stack([stage[pl.ds(512 * a, 512), :].reshape(2, 16, 16, 128).astype(BF16) for a in range(3)], axis=2)

        def scatter(t, carry):
            px, py, pc = partner(t, x, y, core)
            pltpu.make_async_remote_copy(
                src_ref=send.at[b, py // 2, px * 4 + py % 2 * 2 + pc], dst_ref=out_ref.at[b, slot],
                send_sem=out_sem.at[b, 0], recv_sem=out_sem.at[b, 1],
                device_id=device(z, px, py, pc), device_id_type=MESH,
            ).start()
            return carry

        lax.fori_loop(0, 21, scatter, 0)
        lax.fori_loop(22, 32, scatter, 0)
        pltpu.make_async_copy(send.at[b, seg, slot // 2], out_ref.at[b, slot], own_sem.at[b]).start()

    forward(0, 1)
    forward(1, 1)
    forward(2, 1)
    for hop in range(1, 4):
        for c in range(3):
            arrive(c, hop)
            forward(c, hop + 1)
    for c in range(3):
        arrive(c, 4)
        cross(c)

    pltpu.make_async_copy(white.at[pl.ds(0, 31)], white.at[pl.ds(0, 31)], in_sem.at[0]).wait()
    for c in range(3):
        for hop in range(1, 4):
            for way in range(2):
                pass_on(c, hop, way, False).wait_send()
        last_hop(c, False).wait_send()
    for b in range(3):
        pltpu.make_async_copy(send.at[b, seg, slot // 2], out_ref.at[b, slot], own_sem.at[b]).wait()
        whole = out_ref.at[b, pl.ds(0, 31)]
        pltpu.make_async_copy(whole, whole, out_sem.at[b, 1]).wait()
        pltpu.make_async_copy(whole, whole, out_sem.at[b, 0]).wait()


def stacked(records, availability, high, low, places):
    vmem = pl.BlockSpec(memory_space=pltpu.VMEM)
    return pl.pallas_call(
        stack_kernel,
        name="stack",
        out_shape=jax.ShapeDtypeStruct((3, 32, 3, 16, 128), BF16),
        in_specs=[vmem] * 5,
        out_specs=pl.BlockSpec(memory_space=pl.ANY),
        scratch_shapes=[
            pltpu.VMEM((4, 256, 1024), BF16),
            pltpu.VMEM((32, 32, 128), F32),
            pltpu.VMEM((32, 32, 128), BF16),
            pltpu.VMEM((32, 32, 128), BF16),
            pltpu.VMEM((1024, 128), F32),
            pltpu.VMEM((3, 8, 16, 16, 128), BF16),
            pltpu.VMEM((16, 96, 128), BF16),
            pltpu.VMEM((1536, 128), F32),
            pltpu.VMEM((3, 2, 16, 3, 16, 128), BF16),
            pltpu.VMEM((2, 8, 128), F32),
            pltpu.SemaphoreType.DMA((2,)),
            pltpu.SemaphoreType.DMA((2,)),
            pltpu.SemaphoreType.DMA((3, 4, 2)),
            pltpu.SemaphoreType.DMA((3, 4, 2)),
            pltpu.SemaphoreType.DMA((3, 2)),
            pltpu.SemaphoreType.DMA((3,)),
        ],
        compiler_params=pltpu.CompilerParams(
            collective_id=0, has_side_effects=True, vmem_limit_bytes=48 << 20
        ),
    )(records, availability, high, low, places)


def lag_kernel(s_ref, t_ref, out_ref, rows):
    @pl.when(pl.program_id(0) == 0)
    def _():
        for a in range(3):
            for b in range(3):
                block = s_ref[b, :, a].reshape(512, 128).T
                first = 64 * (3 * a + b)
                rows[pl.ds(first, 64), pl.ds(0, 512)] = block[:64]
                rows[pl.ds(first, 64), pl.ds(512, 512)] = block[64:]

    lagged = jnp.dot(rows[...], t_ref[...], preferred_element_type=F32)
    out_ref[...] = lagged.astype(BF16).reshape(9, 64, lagged.shape[1])


def to_lags(stack, table):
    width = 512
    return pl.pallas_call(
        lag_kernel,
        name="lags",
        grid=(2 * LAG // width,),
        out_shape=jax.ShapeDtypeStruct((9, 64, 2 * LAG), BF16),
        in_specs=[
            pl.BlockSpec((3, 32, 3, 16, 128), lambda n: (0, 0, 0, 0, 0)),
            pl.BlockSpec((1024, width), lambda n: (0, n)),
        ],
        out_specs=pl.BlockSpec((9, 64, width), lambda n: (0, 0, n)),
        scratch_shapes=[pltpu.VMEM((576, 1024), BF16)],
        compiler_params=pltpu.CompilerParams(vmem_limit_bytes=40 << 20),
    )(stack, table)


def body(records, availability):
    high, low = forward_table()
    samples = records.shape[-1]
    x = jnp.pad(records.reshape(90, samples), ((0, ROWS - 90), (0, 3072 - samples)))
    stack = stacked(x, availability, jnp.asarray(high), jnp.asarray(low), jnp.asarray(place_table()))
    lagged = to_lags(stack, jnp.asarray(inverse_table()))
    return jnp.transpose(lagged, (1, 0, 2))[None]


def solution(mesh):
    placed = (P("blk", "seg", None, None), P("blk", "seg"))
    return jax.shard_map(
        body, mesh=mesh, in_specs=placed, out_specs=P("blk", "seg", None, None), check_vma=False
    )
```

```python
import functools
import math

import jax
import jax.numpy as jnp
import ml_dtypes
import numpy as np
from jax import lax
from jax.experimental import pallas as pl
from jax.experimental.pallas import tpu as pltpu
from jax.sharding import PartitionSpec as P

MESH = pl.DeviceIdType.MESH
F32 = jnp.float32
BF16 = jnp.bfloat16
NFFT = 4096
FREQS = 512
LAG = 1024
SEGS = 30
ROWS = 90
RESIDUES = ((1, 7), (2, 6), (3, 5), (8, 4))
HALF = math.sqrt(0.5)
SCHEDULE = (
    "F01 F11 F21 A01 F02 A11 F12 A21 F22 A02 F03 A12 F13 A22 F23 "
    "A03 F04 A13 F14 A23 F24 A04 X0 A14 X1 A24 X2"
)
NT = (((1,), (1,)), ((), ()))


def bin_of(p, f):
    return 16 * p + 8 * (f % 2) + np.array(RESIDUES)[f // 4, f // 2 % 2]


def forward_table():
    table = np.zeros((4, 32, 2, 2, 2, 2, 512))
    n = np.arange(512)
    for g in range(4):
        for which in range(2):
            for odd in range(2):
                k = 16 * np.arange(32) + 8 * odd + RESIDUES[g][which]
                angle = (k[:, None] * n[None, :] % NFFT) * (2 * np.pi / NFFT)
                cos, sin = np.cos(angle), np.sin(angle)
                if g == 3:
                    table[g, :, which, odd, 0, which] = cos
                    table[g, :, which, odd, 1, which] = -sin
                else:
                    sign = 1 - 2 * which
                    table[g, :, which, odd, 0, 0] = cos
                    table[g, :, which, odd, 0, 1] = sign * sin
                    table[g, :, which, odd, 1, 0] = -sin
                    table[g, :, which, odd, 1, 1] = sign * cos
    table = table.reshape(4, 256, 1024)
    high = table.astype(ml_dtypes.bfloat16)
    low = (table - high.astype(np.float64)).astype(ml_dtypes.bfloat16)
    return high, low


def inverse_table():
    p, f = np.meshgrid(np.arange(32), np.arange(16), indexing="ij")
    k = bin_of(p, f).reshape(-1)
    tau = np.arange(2 * LAG) - LAG
    angle = (k[:, None] * tau[None, :] % NFFT) * (2 * np.pi / NFFT)
    table = np.concatenate([np.cos(angle), -np.sin(angle)], axis=0) * (2.0 / NFFT)
    return table.astype(ml_dtypes.bfloat16)


def place_table():
    plain = np.zeros((2, 2, 128, 3, 128))
    turned = np.zeros((2, 2, 128, 3, 128))
    for seg in range(2):
        for s in range(SEGS):
            for c in range(3):
                for part in range(2):
                    plain[seg, part, 3 * s + c, c, 64 * part + 30 * seg + s] = 1
                turned[seg, 1, 3 * s + c, c, 30 * seg + s] = 1
                turned[seg, 0, 3 * s + c, c, 64 + 30 * seg + s] = -1
    both = np.stack([plain, turned]).reshape(2, 512, 384)
    return both.astype(ml_dtypes.bfloat16)


def place():
    blk, seg = lax.axis_index("blk"), lax.axis_index("seg")
    z, rest = blk // 16, blk % 16
    return z, rest // 4, seg * 2 + rest // 2 % 2, rest % 2, seg


def device(z, x, y, core):
    return (z * 16 + x * 4 + y % 2 * 2 + core, y // 2)


def partner(t, x, y, core):
    return (x + 2 + t // 8) % 4, (y + 2 + t // 2 % 4) % 4, (core + 1 + t) % 2


def spread(av):
    column = lax.broadcasted_iota(jnp.int32, (SEGS, 128), 1)
    row = lax.broadcasted_iota(jnp.int32, (SEGS, 128), 0)
    pick = ((column >= 3 * row) & (column < 3 * row + 3)).astype(F32)
    return jnp.dot(jnp.broadcast_to(av, (8, SEGS)), pick, preferred_element_type=F32)


def split_rows(w_ref, g, half, value):
    high = value.astype(BF16)
    low = (value - high.astype(F32)).astype(BF16)
    columns = pl.ds(512 * half, 512)
    w_ref[g, pl.ds(0, ROWS), columns] = high
    w_ref[g, pl.ds(128, ROWS), columns] = low


def stack_kernel(
    x_hbm, av_ref, high_hbm, low_hbm, place_hbm, out_ref,
    x_ref, high_ref, low_ref, place_ref,
    w, xs, white, rin, turn, gathered, left, stage, send, counts,
    load_sem, line_sem, core_sem, count_sem, in_sem, ring_send, ring_recv, out_sem, own_sem,
):
    z, x, y, core, seg = place()
    slot = (x * 4 + y % 2 * 2 + core) * 2 + seg
    up, down = (z + 1) % 8, (z + 7) % 8
    barrier = pltpu.get_barrier_semaphore()

    lines = [((x + n) % 4, y, core) for n in range(1, 4)]
    near = [device(z, *at) for at in lines]
    near += [device(z, x, (y + n) % 4, core) for n in range(1, 4)]
    near += [device(z, x, y, 1 - core), device(up, x, y, core), device(down, x, y, core)]
    for other in near:
        pl.semaphore_signal(barrier, inc=1, device_id=other, device_id_type=MESH)

    loads = [
        pltpu.make_async_copy(source, target, load_sem.at[n])
        for n, (source, target) in enumerate(
            ((x_hbm, x_ref), (high_hbm, high_ref), (low_hbm, low_ref), (place_hbm, place_ref))
        )
    ]
    for load in loads:
        load.start()

    own = spread(av_ref[...].astype(F32))
    counts[0] = own
    for g in range(4):
        for start in (80, 208):
            w[g, pl.ds(start, 48), :] = jnp.zeros((48, 1024), BF16)
    loads[0].wait()
    part = [x_ref[:, 0, pl.ds(512 * n, 512)] for n in range(5)]
    part.append(jnp.concatenate([x_ref[:, 0, pl.ds(2560, 440)], jnp.zeros((ROWS, 72), F32)], axis=1))
    d04 = part[0] - part[4]
    d13, s13 = part[1] - part[3], part[1] + part[3]
    split_rows(w, 0, 0, d04 + (d13 - part[5]) * HALF)
    split_rows(w, 0, 1, (part[5] - s13) * HALF - part[2])
    split_rows(w, 1, 0, part[0] + part[4] - part[2])
    split_rows(w, 1, 1, part[3] - part[1] - part[5])
    split_rows(w, 2, 0, d04 + (part[5] - d13) * HALF)
    split_rows(w, 2, 1, (part[5] - s13) * HALF + part[2])
    even, odd = part[0] + part[2] + part[4], s13 + part[5]
    split_rows(w, 3, 0, even + odd)
    split_rows(w, 3, 1, even - odd)

    pl.semaphore_wait(barrier, 9)
    for at in lines:
        pl.semaphore_signal(line_sem, inc=1, device_id=device(z, *at), device_id_type=MESH)
    count_copy = pltpu.make_async_remote_copy(
        src_ref=counts.at[0], dst_ref=counts.at[1], send_sem=count_sem.at[0], recv_sem=count_sem.at[1],
        device_id=device(z, x, (y + 2) % 4, core), device_id_type=MESH,
    )
    count_copy.start()

    power = jnp.zeros((32, 8, 128), F32)
    loads[1].wait()
    loads[2].wait()
    for g in range(4):
        if g == 2:
            pl.semaphore_wait(line_sem, 3)
            pl.semaphore_signal(core_sem, inc=1, device_id=device(z, x, y, 1 - core), device_id_type=MESH)
        high = lax.dot_general(high_ref[g], w[g], NT, preferred_element_type=F32)
        low = lax.dot_general(low_ref[g], w[g], NT, preferred_element_type=F32)
        both = high + low
        value = (both[:, :128] + both[:, 128:]).reshape(32, 8, 128)
        xs[:, pl.ds(8 * g, 8), :] = value
        power = power + value * value
    power = jnp.sum(power.reshape(16, 16, 128), axis=1)
    triple = power + pltpu.roll(power, 127, 1) + pltpu.roll(power, 126, 1)
    phase = lax.broadcasted_iota(jnp.int32, (16, 128), 1) % 3
    total = jnp.where(phase == 0, triple, jnp.where(phase == 1, pltpu.roll(triple, 1, 1), pltpu.roll(triple, 2, 1)))
    amplitude = jnp.sqrt(total * (1.0 / 96) + 1e-06)
    count_copy.wait()
    count = (jnp.sum(own, axis=1, keepdims=True) + jnp.sum(counts[1], axis=1, keepdims=True)) * (1.0 / 3)
    weight = own / jnp.sqrt(jnp.round(count))
    factor = weight[0:1] / amplitude
    white[...] = (xs[...].reshape(16, 64, 128) * factor[:, None, :]).reshape(32, 32, 128).astype(BF16)

    pl.semaphore_wait(core_sem, 1)

    def scatter(t, carry):
        px, py, pc = partner(t, x, y, core)
        target = (px * 4 + py % 2 * 2 + pc) * 2 + py // 2
        pltpu.make_async_remote_copy(
            src_ref=white.at[target], dst_ref=rin.at[slot], send_sem=in_sem.at[0], recv_sem=in_sem.at[1],
            device_id=device(z, px, py, pc), device_id_type=MESH,
        ).start()
        return carry

    lax.fori_loop(0, 21, scatter, 0)
    lax.fori_loop(22, 32, scatter, 0)
    pltpu.make_async_copy(rin.at[pl.ds(0, 31)], rin.at[pl.ds(0, 31)], in_sem.at[1]).wait()
    rin[slot] = white[slot]

    def swap(source, carry):
        start = source % 2 * 512 + source // 2
        turn[pl.ds(start, 32, stride=16), :] = rin[source].astype(F32)
        return carry

    lax.fori_loop(0, 32, swap, 0)
    loads[3].wait()
    pieces = turn[...].reshape(2, 16, 2, 16, 128)
    rows = jnp.concatenate(
        [pieces[s, :, part].reshape(256, 128).astype(BF16) for s in range(2) for part in range(2)], axis=1
    )
    plain = jnp.dot(rows, place_ref[0], preferred_element_type=F32).astype(BF16)
    turned = jnp.dot(rows, place_ref[1], preferred_element_type=F32).astype(BF16)
    for c in range(3):
        one = plain[:, 128 * c : 128 * (c + 1)].reshape(16, 16, 128)
        gathered[c, z] = one
        left[:, pl.ds(16 * c, 16), :] = one
        left[:, pl.ds(48 + 16 * c, 16), :] = turned[:, 128 * c : 128 * (c + 1)].reshape(16, 16, 128)

    def pass_on(c, hop, way, start):
        source = (z + 9 - hop) % 8 if way == 0 else (z + hop - 1) % 8
        copy = pltpu.make_async_remote_copy(
            src_ref=gathered.at[c, source], dst_ref=gathered.at[c, source],
            send_sem=ring_send.at[c, hop - 1, way], recv_sem=ring_recv.at[c, hop - 1, way],
            device_id=device(up if way == 0 else down, x, y, core), device_id_type=MESH,
        )
        if start:
            copy.start()
        return copy

    def last_hop(c, start):
        source = (z + 5 + 6 * core) % 8
        copy = pltpu.make_async_remote_copy(
            src_ref=gathered.at[c, source], dst_ref=gathered.at[c, source],
            send_sem=ring_send.at[c, 3, 0], recv_sem=ring_recv.at[c, 3, 0],
            device_id=device((z + 1 + 6 * core) % 8, x, y, core), device_id_type=MESH,
        )
        if start:
            copy.start()
        return copy

    def arrive(c, hop):
        if hop == 4:
            last_hop(c, False).wait_recv()
        else:
            for way in range(2):
                pass_on(c, hop, way, False).wait_recv()

    def forward(c, hop):
        if hop == 4:
            last_hop(c, True)
        else:
            for way in range(2):
                pass_on(c, hop, way, True)

    lane = lax.broadcasted_iota(jnp.int32, (16, 128), 1) < 64

    def cross(b):
        def four_bins(step, carry):
            for f in [4 * step + n for n in range(4)]:
                right = gathered[b, :, f].reshape(128, 128)
                product = lax.dot_general(left[f], right, NT, preferred_element_type=F32)
                for a in range(3):
                    re = product[16 * a : 16 * (a + 1)]
                    im = product[48 + 16 * a : 48 + 16 * (a + 1)]
                    mixed = pltpu.roll(jnp.where(lane, im, re), 64, 1)
                    stage[pl.ds(512 * a + f, 16, stride=16), :] = jnp.where(lane, re, mixed)
                    stage[pl.ds(512 * a + 256 + f, 16, stride=16), :] = jnp.where(lane, mixed, im)
            return carry

        lax.fori_loop(0, 4, four_bins, 0)
        send[b] = jnp.stack([stage[pl.ds(512 * a, 512), :].reshape(2, 16, 16, 128).astype(BF16) for a in range(3)], axis=2)

        def scatter(t, carry):
            px, py, pc = partner(t, x, y, core)
            pltpu.make_async_remote_copy(
                src_ref=send.at[b, py // 2, px * 4 + py % 2 * 2 + pc], dst_ref=out_ref.at[b, slot],
                send_sem=out_sem.at[b, 0], recv_sem=out_sem.at[b, 1],
                device_id=device(z, px, py, pc), device_id_type=MESH,
            ).start()
            return carry

        lax.fori_loop(0, 21, scatter, 0)
        lax.fori_loop(22, 32, scatter, 0)
        pltpu.make_async_copy(send.at[b, seg, slot // 2], out_ref.at[b, slot], own_sem.at[b]).start()

    steps = {"F": forward, "A": arrive, "X": cross}
    for step in SCHEDULE.split():
        steps[step[0]](*(int(digit) for digit in step[1:]))

    pltpu.make_async_copy(white.at[pl.ds(0, 31)], white.at[pl.ds(0, 31)], in_sem.at[0]).wait()
    for c in range(3):
        for hop in range(1, 4):
            for way in range(2):
                pass_on(c, hop, way, False).wait_send()
        last_hop(c, False).wait_send()
    for b in range(3):
        pltpu.make_async_copy(send.at[b, seg, slot // 2], out_ref.at[b, slot], own_sem.at[b]).wait()
        whole = out_ref.at[b, pl.ds(0, 31)]
        pltpu.make_async_copy(whole, whole, out_sem.at[b, 1]).wait()
        pltpu.make_async_copy(whole, whole, out_sem.at[b, 0]).wait()


def stacked(records, availability, high, low, places):
    vmem, hbm = pl.BlockSpec(memory_space=pltpu.VMEM), pl.BlockSpec(memory_space=pl.ANY)
    return pl.pallas_call(
        stack_kernel,
        name="stack",
        out_shape=jax.ShapeDtypeStruct((3, 32, 3, 16, 128), BF16),
        in_specs=[hbm, vmem, hbm, hbm, hbm],
        out_specs=hbm,
        scratch_shapes=[
            pltpu.VMEM(records.shape, F32),
            pltpu.VMEM(high.shape, BF16),
            pltpu.VMEM(low.shape, BF16),
            pltpu.VMEM(places.shape, BF16),
            pltpu.VMEM((4, 256, 1024), BF16),
            pltpu.VMEM((32, 32, 128), F32),
            pltpu.VMEM((32, 32, 128), BF16),
            pltpu.VMEM((32, 32, 128), BF16),
            pltpu.VMEM((1024, 128), F32),
            pltpu.VMEM((3, 8, 16, 16, 128), BF16),
            pltpu.VMEM((16, 96, 128), BF16),
            pltpu.VMEM((1536, 128), F32),
            pltpu.VMEM((3, 2, 16, 3, 16, 128), BF16),
            pltpu.VMEM((2, 8, 128), F32),
            pltpu.SemaphoreType.DMA((4,)),
            pltpu.SemaphoreType.REGULAR,
            pltpu.SemaphoreType.REGULAR,
            pltpu.SemaphoreType.DMA((2,)),
            pltpu.SemaphoreType.DMA((2,)),
            pltpu.SemaphoreType.DMA((3, 4, 2)),
            pltpu.SemaphoreType.DMA((3, 4, 2)),
            pltpu.SemaphoreType.DMA((3, 2)),
            pltpu.SemaphoreType.DMA((3,)),
        ],
        compiler_params=pltpu.CompilerParams(
            collective_id=0, has_side_effects=True, vmem_limit_bytes=62 << 20
        ),
    )(records, availability, high, low, places)


def lag_kernel(s_ref, t_ref, out_ref, rows):
    @pl.when(pl.program_id(0) == 0)
    def _():
        for a in range(3):
            for b in range(3):
                block = s_ref[b, :, a].reshape(512, 128).T
                first = 64 * (3 * a + b)
                rows[pl.ds(first, 64), pl.ds(0, 512)] = block[:64]
                rows[pl.ds(first, 64), pl.ds(512, 512)] = block[64:]

    lagged = jnp.dot(rows[...], t_ref[...], preferred_element_type=F32)
    out_ref[...] = lagged.astype(BF16).reshape(9, 64, lagged.shape[1])


def to_lags(stack, table):
    width = 512
    return pl.pallas_call(
        lag_kernel,
        name="lags",
        grid=(2 * LAG // width,),
        out_shape=jax.ShapeDtypeStruct((9, 64, 2 * LAG), BF16),
        in_specs=[
            pl.BlockSpec((3, 32, 3, 16, 128), lambda n: (0, 0, 0, 0, 0)),
            pl.BlockSpec((1024, width), lambda n: (0, n)),
        ],
        out_specs=pl.BlockSpec((9, 64, width), lambda n: (0, 0, n)),
        scratch_shapes=[pltpu.VMEM((576, 1024), BF16)],
        compiler_params=pltpu.CompilerParams(vmem_limit_bytes=62 << 20),
    )(stack, table)


def body(records, availability):
    high, low = forward_table()
    samples = records.shape[-1]
    x = records.reshape(ROWS, 1, samples)
    stack = stacked(x, availability, jnp.asarray(high), jnp.asarray(low), jnp.asarray(place_table()))
    lagged = to_lags(stack, jnp.asarray(inverse_table()))
    return jnp.transpose(lagged, (1, 0, 2))[None]


def solution(mesh):
    placed = (P("blk", "seg", None, None), P("blk", "seg"))
    return jax.shard_map(
        body, mesh=mesh, in_specs=placed, out_specs=P("blk", "seg", None, None), check_vma=False
    )
```

```python
import functools
import math

import jax
import jax.numpy as jnp
import ml_dtypes
import numpy as np
from jax import lax
from jax.experimental import pallas as pl
from jax.experimental.pallas import tpu as pltpu
from jax.sharding import PartitionSpec as P

MESH = pl.DeviceIdType.MESH
F32 = jnp.float32
BF16 = jnp.bfloat16
NFFT = 4096
FREQS = 512
LAG = 1024
SEGS = 30
ROWS = 90
RESIDUES = ((1, 7), (2, 6), (3, 5), (8, 4))
HALF = math.sqrt(0.5)
HALVES = 1
OTHERS = sorted(
    ((dx, dy, dc) for dx in range(4) for dy in range(4) for dc in range(2) if dx or dy or dc),
    key=lambda d: (-min(d[0], 4 - d[0]) - min(d[1], 4 - d[1]), (5 * d[0] + 3 * d[1] + d[2]) % 7),
)
SCHEDULE = (
    ["F010", "F110", "F210", "A01", "F021", "A11", "F121", "A21", "F221"]
    + ["A02", "F032", "F042", "A12", "F132", "F142", "A22", "F232", "F242"]
    + ["A03", "A04", "C0", "S00", "S01", "S02", "S03"]
    + ["A13", "A14", "C1", "S10", "S11", "S12", "S13"]
    + ["A23", "A24", "C2", "S20", "S21", "S22", "S23"]
)
NT = (((1,), (1,)), ((), ()))


def bin_of(p, f):
    return 16 * p + 8 * (f % 2) + np.array(RESIDUES)[f // 4, f // 2 % 2]


def forward_table():
    table = np.zeros((4, 32, 2, 2, 2, 2, 512))
    n = np.arange(512)
    for g in range(4):
        for which in range(2):
            for odd in range(2):
                k = 16 * np.arange(32) + 8 * odd + RESIDUES[g][which]
                angle = (k[:, None] * n[None, :] % NFFT) * (2 * np.pi / NFFT)
                cos, sin = np.cos(angle), np.sin(angle)
                if g == 3:
                    table[g, :, which, odd, 0, which] = cos
                    table[g, :, which, odd, 1, which] = -sin
                else:
                    sign = 1 - 2 * which
                    table[g, :, which, odd, 0, 0] = cos
                    table[g, :, which, odd, 0, 1] = sign * sin
                    table[g, :, which, odd, 1, 0] = -sin
                    table[g, :, which, odd, 1, 1] = sign * cos
    table = table.reshape(4, 256, 1024)
    high = table.astype(ml_dtypes.bfloat16)
    low = (table - high.astype(np.float64)).astype(ml_dtypes.bfloat16)
    return high.reshape(1024, 1024), low.reshape(1024, 1024)


def inverse_table():
    p, f = np.meshgrid(np.arange(32), np.arange(16), indexing="ij")
    k = bin_of(p, f).reshape(-1)
    tau = np.arange(2 * LAG) - LAG
    angle = (k[:, None] * tau[None, :] % NFFT) * (2 * np.pi / NFFT)
    table = np.concatenate([np.cos(angle), -np.sin(angle)], axis=0) * (2.0 / NFFT)
    return table.astype(ml_dtypes.bfloat16)


def place_table():
    plain = np.zeros((2, 2, 128, 4, 128))
    turned = np.zeros((2, 2, 128, 4, 128))
    for seg in range(2):
        for s in range(SEGS):
            for c in range(3):
                for part in range(2):
                    plain[seg, part, 3 * s + c, c, 64 * part + 30 * seg + s] = 1
                turned[seg, 1, 3 * s + c, c, 30 * seg + s] = 1
                turned[seg, 0, 3 * s + c, c, 64 + 30 * seg + s] = -1
    both = np.concatenate([plain.reshape(512, 512), turned.reshape(512, 512)], axis=1)
    return both.astype(ml_dtypes.bfloat16)


def all_tables(inverse):
    return np.concatenate([*forward_table(), inverse[:, :LAG], inverse[:, LAG:], place_table()], axis=0)


def place():
    blk, seg = lax.axis_index("blk"), lax.axis_index("seg")
    z, rest = blk // 16, blk % 16
    return z, rest // 4, seg * 2 + rest // 2 % 2, rest % 2, seg


def device(z, x, y, core):
    return (z * 16 + x * 4 + y % 2 * 2 + core, y // 2)


def lag_rows(blocks):
    turned = [block.T for block in blocks]
    return jnp.concatenate([jnp.concatenate([one[:64], one[64:]], axis=1) for one in turned], axis=0)


def spread(av):
    column = lax.broadcasted_iota(jnp.int32, (SEGS, 128), 1)
    row = lax.broadcasted_iota(jnp.int32, (SEGS, 128), 0)
    pick = ((column >= 3 * row) & (column < 3 * row + 3)).astype(F32)
    return jnp.dot(jnp.broadcast_to(av, (8, SEGS)), pick, preferred_element_type=F32)


def split_rows(w_ref, g, half, value):
    high = value.astype(BF16)
    low = (value - high.astype(F32)).astype(BF16)
    columns = pl.ds(512 * half, 512)
    w_ref[g, pl.ds(0, ROWS), columns] = high
    w_ref[g, pl.ds(128, ROWS), columns] = low


def stack_kernel(
    x_hbm, av_ref, table_hbm, last_ref, lags,
    x_ref, table_ref, stacks,
    w, xs, white, rin, turn, gathered, left, stage, send, counts,
    load_sem, line_sem, core_sem, count_sem, in_sem, ring_send, ring_recv, out_sem, own_sem,
):
    z, x, y, core, seg = place()
    slot = (x * 4 + y % 2 * 2 + core) * 2 + seg
    others = [((x + dx) % 4, (y + dy) % 4, (core + dc) % 2) for dx, dy, dc in OTHERS]
    barrier = pltpu.get_barrier_semaphore()

    lines = [((x + n) % 4, y, core) for n in range(1, 4)]
    near = [device(z, *at) for at in lines]
    near += [device(z, x, (y + n) % 4, core) for n in range(1, 4)]
    near += [device(z, x, y, 1 - core)]
    near += [device((z + n) % 8, x, y, core) for n in (1, 2, 6, 7)]
    for other in near:
        pl.semaphore_signal(barrier, inc=1, device_id=other, device_id_type=MESH)

    parts = [pl.ds(first, rows) for first, rows in ((0, 1024), (1024, 1024), (4096, 512), (2048, 2048))]
    loads = [pltpu.make_async_copy(x_hbm, x_ref, load_sem.at[4])]
    loads += [
        pltpu.make_async_copy(table_hbm.at[rows], table_ref.at[rows], load_sem.at[n]) for n, rows in enumerate(parts)
    ]
    for load in loads:
        load.start()

    own = spread(av_ref[...].astype(F32))
    counts[0] = own
    for g in range(4):
        for start in (80, 208):
            w[g, pl.ds(start, 48), :] = jnp.zeros((48, 1024), BF16)
    loads[0].wait()
    part = [x_ref[:, 0, pl.ds(512 * n, 512)] for n in range(5)]
    part.append(jnp.concatenate([x_ref[:, 0, pl.ds(2560, 440)], jnp.zeros((ROWS, 72), F32)], axis=1))
    d04 = part[0] - part[4]
    d13, s13 = part[1] - part[3], part[1] + part[3]
    split_rows(w, 0, 0, d04 + (d13 - part[5]) * HALF)
    split_rows(w, 0, 1, (part[5] - s13) * HALF - part[2])
    split_rows(w, 1, 0, part[0] + part[4] - part[2])
    split_rows(w, 1, 1, part[3] - part[1] - part[5])
    split_rows(w, 2, 0, d04 + (part[5] - d13) * HALF)
    split_rows(w, 2, 1, (part[5] - s13) * HALF + part[2])
    even, odd = part[0] + part[2] + part[4], s13 + part[5]
    split_rows(w, 3, 0, even + odd)
    split_rows(w, 3, 1, even - odd)

    pl.semaphore_wait(barrier, 11)
    for at in lines:
        pl.semaphore_signal(line_sem, inc=1, device_id=device(z, *at), device_id_type=MESH)
    count_copy = pltpu.make_async_remote_copy(
        src_ref=counts.at[0], dst_ref=counts.at[1], send_sem=count_sem.at[0], recv_sem=count_sem.at[1],
        device_id=device(z, x, (y + 2) % 4, core), device_id_type=MESH,
    )
    count_copy.start()

    power = jnp.zeros((32, 8, 128), F32)
    loads[1].wait()
    loads[2].wait()
    for g in range(4):
        if g == 2:
            pl.semaphore_wait(line_sem, 3)
            pl.semaphore_signal(core_sem, inc=1, device_id=device(z, x, y, 1 - core), device_id_type=MESH)
        high = lax.dot_general(table_ref[256 * g : 256 * (g + 1)], w[g], NT, preferred_element_type=F32)
        low = lax.dot_general(table_ref[1024 + 256 * g : 1280 + 256 * g], w[g], NT, preferred_element_type=F32)
        both = high + low
        value = (both[:, :128] + both[:, 128:]).reshape(32, 8, 128)
        xs[:, pl.ds(8 * g, 8), :] = value
        power = power + value * value
    power = jnp.sum(power.reshape(16, 16, 128), axis=1)
    triple = power + pltpu.roll(power, 127, 1) + pltpu.roll(power, 126, 1)
    phase = lax.broadcasted_iota(jnp.int32, (16, 128), 1) % 3
    total = jnp.where(phase == 0, triple, jnp.where(phase == 1, pltpu.roll(triple, 1, 1), pltpu.roll(triple, 2, 1)))
    amplitude = jnp.sqrt(total * (1.0 / 96) + 1e-06)
    count_copy.wait()
    count = (jnp.sum(own, axis=1, keepdims=True) + jnp.sum(counts[1], axis=1, keepdims=True)) * (1.0 / 3)
    weight = own / jnp.sqrt(jnp.round(count))
    factor = weight[0:1] / amplitude
    white[...] = (xs[...].reshape(16, 64, 128) * factor[:, None, :]).reshape(32, 32, 128).astype(BF16)

    pl.semaphore_wait(core_sem, 1)

    for px, py, pc in others:
        target = (px * 4 + py % 2 * 2 + pc) * 2 + py // 2
        pltpu.make_async_remote_copy(
            src_ref=white.at[target], dst_ref=rin.at[slot], send_sem=in_sem.at[0], recv_sem=in_sem.at[1],
            device_id=device(z, px, py, pc), device_id_type=MESH,
        ).start()
    pltpu.make_async_copy(rin.at[pl.ds(0, 31)], rin.at[pl.ds(0, 31)], in_sem.at[1]).wait()
    rin[slot] = white[slot]

    def swap(source, carry):
        start = source % 2 * 512 + source // 2
        turn[pl.ds(start, 32, stride=16), :] = rin[source].astype(F32)
        return carry

    lax.fori_loop(0, 32, swap, 0)
    loads[3].wait()
    pieces = turn[...].reshape(2, 16, 2, 16, 128)
    rows = jnp.concatenate(
        [pieces[s, :, part].reshape(256, 128).astype(BF16) for s in range(2) for part in range(2)], axis=1
    )
    plain = jnp.dot(rows, table_ref[4096:, :384], preferred_element_type=F32).astype(BF16)
    turned = jnp.dot(rows, table_ref[4096:, 512:896], preferred_element_type=F32).astype(BF16)
    for c in range(3):
        one = plain[:, 128 * c : 128 * (c + 1)].reshape(16, 16, 128)
        gathered[c, z] = one
        left[:, pl.ds(16 * c, 16), :] = one
        left[:, pl.ds(48 + 16 * c, 16), :] = turned[:, 128 * c : 128 * (c + 1)].reshape(16, 16, 128)

    def moves(u, reach, come):
        size = 16 // HALVES
        signs = (1, -1) if reach < 4 else (1 - 2 * core,)
        for way, sign in enumerate(signs):
            piece = gathered.at[u // HALVES, (z + 8 - sign * come) % 8, pl.ds(u % HALVES * size, size)]
            yield pltpu.make_async_remote_copy(
                src_ref=piece, dst_ref=piece,
                send_sem=ring_send.at[u, reach - 1, way], recv_sem=ring_recv.at[u, reach - 1, way],
                device_id=device((z + 8 + sign * (reach - come)) % 8, x, y, core), device_id_type=MESH,
            )

    def forward(u, reach, come):
        for copy in moves(u, reach, come):
            copy.start()

    def arrive(u, reach):
        for copy in moves(u, reach, 0):
            copy.wait_recv()

    lane = lax.broadcasted_iota(jnp.int32, (16, 128), 1) < 64

    def cross(b):
        def four_bins(step, carry):
            for f in [4 * step + n for n in range(4)]:
                right = gathered[b, :, f].reshape(128, 128)
                product = lax.dot_general(left[f], right, NT, preferred_element_type=F32)
                for a in range(3):
                    re = product[16 * a : 16 * (a + 1)]
                    im = product[48 + 16 * a : 48 + 16 * (a + 1)]
                    mixed = pltpu.roll(jnp.where(lane, im, re), 64, 1)
                    stage[pl.ds(512 * a + f, 16, stride=16), :] = jnp.where(lane, re, mixed)
                    stage[pl.ds(512 * a + 256 + f, 16, stride=16), :] = jnp.where(lane, mixed, im)
            return carry

        lax.fori_loop(0, 4, four_bins, 0)
        send[b] = jnp.stack([stage[pl.ds(512 * a, 512), :].reshape(2, 16, 16, 128).astype(BF16) for a in range(3)], axis=2)

    def keep(b):
        target = stacks.at[b, slot] if b < 2 else last_ref.at[slot]
        return pltpu.make_async_copy(send.at[b, seg, slot // 2], target, own_sem.at[b])

    def ship(b, quarter):
        for px, py, pc in others[8 * quarter : 8 * quarter + 8]:
            pltpu.make_async_remote_copy(
                src_ref=send.at[b, py // 2, px * 4 + py % 2 * 2 + pc], dst_ref=stacks.at[b, slot] if b < 2 else last_ref.at[slot],
                send_sem=out_sem.at[b, 0], recv_sem=out_sem.at[b, 1],
                device_id=device(z, px, py, pc), device_id_type=MESH,
            ).start()
        if quarter == 3:
            keep(b).start()

    steps = {"F": forward, "A": arrive, "C": cross, "S": ship}
    for step in SCHEDULE:
        steps[step[0]](*(int(digit) for digit in step[1:]))

    loads[4].wait()
    for b in range(2):
        keep(b).wait()
        whole = stacks.at[b, pl.ds(0, 31)]
        pltpu.make_async_copy(whole, whole, out_sem.at[b, 1]).wait()
        rows = lag_rows([stacks[b, :, a].reshape(512, 128) for a in range(3)])
        for n in range(4):
            half = table_ref[2048 + 1024 * (n // 2) : 3072 + 1024 * (n // 2), 512 * (n % 2) : 512 * (n % 2 + 1)]
            lagged = jnp.dot(rows, half, preferred_element_type=F32)
            lags[b, :, :, pl.ds(512 * n, 512)] = lagged.astype(BF16).reshape(3, 64, 512)

    pltpu.make_async_copy(white.at[pl.ds(0, 31)], white.at[pl.ds(0, 31)], in_sem.at[0]).wait()
    for u in range(3 * HALVES):
        for reach in range(1, 5):
            for copy in moves(u, reach, 0):
                copy.wait_send()
    keep(2).wait()
    whole = last_ref.at[pl.ds(0, 31)]
    pltpu.make_async_copy(whole, whole, out_sem.at[2, 1]).wait()
    for b in range(3):
        pltpu.make_async_copy(whole, whole, out_sem.at[b, 0]).wait()


def in_hbm(array):
    return pltpu.with_memory_space_constraint(array, pltpu.HBM)


def stacked(records, availability, tables):
    vmem, hbm = pl.BlockSpec(memory_space=pltpu.VMEM), pl.BlockSpec(memory_space=pl.ANY)
    return pl.pallas_call(
        stack_kernel,
        name="stack",
        out_shape=(
            pltpu.VMEM((32, 3, 16, 128), BF16),
            pltpu.VMEM((2, 3, 64, 2 * LAG), BF16),
        ),
        in_specs=[hbm, vmem, hbm],
        out_specs=(vmem, vmem),
        scratch_shapes=[
            pltpu.VMEM(records.shape, F32),
            pltpu.VMEM(tables.shape, BF16),
            pltpu.VMEM((2, 32, 3, 16, 128), BF16),
            pltpu.VMEM((4, 256, 1024), BF16),
            pltpu.VMEM((32, 32, 128), F32),
            pltpu.VMEM((32, 32, 128), BF16),
            pltpu.VMEM((32, 32, 128), BF16),
            pltpu.VMEM((1024, 128), F32),
            pltpu.VMEM((3, 8, 16, 16, 128), BF16),
            pltpu.VMEM((16, 96, 128), BF16),
            pltpu.VMEM((1536, 128), F32),
            pltpu.VMEM((3, 2, 16, 3, 16, 128), BF16),
            pltpu.VMEM((2, 8, 128), F32),
            pltpu.SemaphoreType.DMA((5,)),
            pltpu.SemaphoreType.REGULAR,
            pltpu.SemaphoreType.REGULAR,
            pltpu.SemaphoreType.DMA((2,)),
            pltpu.SemaphoreType.DMA((2,)),
            pltpu.SemaphoreType.DMA((3 * HALVES, 4, 2)),
            pltpu.SemaphoreType.DMA((3 * HALVES, 4, 2)),
            pltpu.SemaphoreType.DMA((3, 2)),
            pltpu.SemaphoreType.DMA((3,)),
        ],
        compiler_params=pltpu.CompilerParams(
            collective_id=0, has_side_effects=True, vmem_limit_bytes=40 << 20
        ),
    )(in_hbm(records), in_hbm(availability), in_hbm(tables))


def lag_kernel(last_ref, part_ref, table_ref, out_hbm, lags, part_sem, out_sem):
    copies = [
        pltpu.make_async_copy(part_ref.at[b, a], out_hbm.at[3 * a + b], part_sem.at[b, a])
        for b in range(2)
        for a in range(3)
    ]
    for copy in copies:
        copy.start()
    rows = lag_rows([last_ref[:, a].reshape(512, 128) for a in range(3)])
    for n in range(4):
        column = pl.ds(512 * n, 512)
        lagged = jnp.dot(rows, table_ref[:, column], preferred_element_type=F32)
        lags[:, :, column] = lagged.astype(BF16).reshape(3, 64, 512)
        for a in range(3):
            copies.append(
                pltpu.make_async_copy(
                    lags.at[a, :, column], out_hbm.at[3 * a + 2, :, column], out_sem.at[n, a]
                )
            )
            copies[-1].start()
    for copy in copies:
        copy.wait()


def to_lags(last, part, table):
    vmem = pl.BlockSpec(memory_space=pltpu.VMEM)
    return pl.pallas_call(
        lag_kernel,
        name="lags",
        out_shape=jax.ShapeDtypeStruct((9, 64, 2 * LAG), BF16),
        in_specs=[vmem] * 3,
        out_specs=pl.BlockSpec(memory_space=pl.ANY),
        scratch_shapes=[
            pltpu.VMEM((3, 64, 2 * LAG), BF16),
            pltpu.SemaphoreType.DMA((2, 3)),
            pltpu.SemaphoreType.DMA((4, 3)),
        ],
        compiler_params=pltpu.CompilerParams(vmem_limit_bytes=40 << 20),
    )(*(pltpu.with_memory_space_constraint(array, pltpu.VMEM) for array in (last, part, table)))


def body(records, availability):
    samples = records.shape[-1]
    inverse = inverse_table()
    last, part = stacked(records.reshape(ROWS, 1, samples), availability, jnp.asarray(all_tables(inverse)))
    lagged = to_lags(last, part, jnp.asarray(inverse))
    return jnp.transpose(lagged, (1, 0, 2))[None]


def solution(mesh):
    placed = (P("blk", "seg", None, None), P("blk", "seg"))
    return jax.shard_map(
        body, mesh=mesh, in_specs=placed, out_specs=P("blk", "seg", None, None), check_vma=False
    )
```

```python
import functools
import math

import jax
import jax.numpy as jnp
import ml_dtypes
import numpy as np
from jax import lax
from jax.experimental import pallas as pl
from jax.experimental.pallas import tpu as pltpu
from jax.sharding import PartitionSpec as P

MESH = pl.DeviceIdType.MESH
F32 = jnp.float32
BF16 = jnp.bfloat16
NFFT = 4096
FREQS = 512
LAG = 1024
SEGS = 30
ROWS = 90
RESIDUES = ((1, 7), (2, 6), (3, 5), (8, 4))
HALF = math.sqrt(0.5)
HALVES = 1
OTHERS = sorted(
    ((dx, dy, dc) for dx in range(4) for dy in range(4) for dc in range(2) if dx or dy or dc),
    key=lambda d: (-min(d[0], 4 - d[0]) - min(d[1], 4 - d[1]), (5 * d[0] + 3 * d[1] + d[2]) % 7),
)
SCHEDULE = (
    ["F010", "F110", "L", "A01", "F021", "F210", "A11", "F121", "A02", "F032", "F042"]
    + ["A21", "F221", "A12", "F132", "F142", "A03", "A04", "C0"]
    + ["S00", "S01", "A22", "F232", "F242", "S02", "S03"]
    + ["A13", "A14", "C1", "S10", "S11", "S12", "S13"]
    + ["A23", "A24", "C2", "S20", "S21", "S22", "S23"]
)
NT = (((1,), (1,)), ((), ()))


def bin_of(p, f):
    return 16 * p + 8 * (f % 2) + np.array(RESIDUES)[f // 4, f // 2 % 2]


def forward_table():
    table = np.zeros((4, 32, 2, 2, 2, 2, 512))
    n = np.arange(512)
    for g in range(4):
        for which in range(2):
            for odd in range(2):
                k = 16 * np.arange(32) + 8 * odd + RESIDUES[g][which]
                angle = (k[:, None] * n[None, :] % NFFT) * (2 * np.pi / NFFT)
                cos, sin = np.cos(angle), np.sin(angle)
                if g == 3:
                    table[g, :, which, odd, 0, which] = cos
                    table[g, :, which, odd, 1, which] = -sin
                else:
                    sign = 1 - 2 * which
                    table[g, :, which, odd, 0, 0] = cos
                    table[g, :, which, odd, 0, 1] = sign * sin
                    table[g, :, which, odd, 1, 0] = -sin
                    table[g, :, which, odd, 1, 1] = sign * cos
    table = table.reshape(4, 256, 1024)
    high = table.astype(ml_dtypes.bfloat16)
    low = (table - high.astype(np.float64)).astype(ml_dtypes.bfloat16)
    return high.reshape(1024, 1024), low.reshape(1024, 1024)


def inverse_table():
    p, f = np.meshgrid(np.arange(32), np.arange(16), indexing="ij")
    k = bin_of(p, f).reshape(-1)
    tau = np.arange(2 * LAG) - LAG
    angle = (k[:, None] * tau[None, :] % NFFT) * (2 * np.pi / NFFT)
    table = np.concatenate([np.cos(angle), -np.sin(angle)], axis=0) * (2.0 / NFFT)
    return table.astype(ml_dtypes.bfloat16)


def place_table():
    plain = np.zeros((2, 2, 128, 4, 128))
    turned = np.zeros((2, 2, 128, 4, 128))
    for seg in range(2):
        for s in range(SEGS):
            for c in range(3):
                for part in range(2):
                    plain[seg, part, 3 * s + c, c, 64 * part + 30 * seg + s] = 1
                turned[seg, 1, 3 * s + c, c, 30 * seg + s] = 1
                turned[seg, 0, 3 * s + c, c, 64 + 30 * seg + s] = -1
    both = np.concatenate([plain.reshape(512, 512), turned.reshape(512, 512)], axis=1)
    return both.astype(ml_dtypes.bfloat16)


def all_tables(inverse):
    return np.concatenate([*forward_table(), inverse[:, :LAG], inverse[:, LAG:], place_table()], axis=0)


def place():
    blk, seg = lax.axis_index("blk"), lax.axis_index("seg")
    z, rest = blk // 16, blk % 16
    return z, rest // 4, seg * 2 + rest // 2 % 2, rest % 2, seg


def device(z, x, y, core):
    return (z * 16 + x * 4 + y % 2 * 2 + core, y // 2)


def lag_rows(blocks):
    turned = [block.T for block in blocks]
    return jnp.concatenate([jnp.concatenate([one[:64], one[64:]], axis=1) for one in turned], axis=0)


def spread(av):
    column = lax.broadcasted_iota(jnp.int32, (SEGS, 128), 1)
    row = lax.broadcasted_iota(jnp.int32, (SEGS, 128), 0)
    pick = ((column >= 3 * row) & (column < 3 * row + 3)).astype(F32)
    return jnp.dot(jnp.broadcast_to(av, (8, SEGS)), pick, preferred_element_type=F32)


def split_rows(w_ref, g, half, value):
    high = value.astype(BF16)
    low = (value - high.astype(F32)).astype(BF16)
    columns = pl.ds(512 * half, 512)
    w_ref[g, pl.ds(0, ROWS), columns] = high
    w_ref[g, pl.ds(128, ROWS), columns] = low


def stack_kernel(
    x_hbm, av_hbm, table_hbm, last_ref, lags,
    x_ref, av_ref, table_ref, stacks,
    w, xs, white, rin, turn, gathered, left, stage, send, counts,
    load_sem, line_sem, core_sem, count_sem, in_sem, ring_send, ring_recv, out_sem, own_sem,
):
    z, x, y, core, seg = place()
    slot = (x * 4 + y % 2 * 2 + core) * 2 + seg
    others = [((x + dx) % 4, (y + dy) % 4, (core + dc) % 2) for dx, dy, dc in OTHERS]
    parts = [pl.ds(first, rows) for first, rows in ((0, 1024), (1024, 1024), (4096, 512), (2048, 2048))]
    loads = [pltpu.make_async_copy(x_hbm, x_ref, load_sem.at[4]), pltpu.make_async_copy(av_hbm, av_ref, load_sem.at[5])]
    loads += [
        pltpu.make_async_copy(table_hbm.at[rows], table_ref.at[rows], load_sem.at[n]) for n, rows in enumerate(parts)
    ]
    for load in loads:
        load.start()

    barrier = pltpu.get_barrier_semaphore()

    lines = [((x + n) % 4, y, core) for n in range(1, 4)]
    near = [device(z, x, (y + n) % 4, core) for n in (2, 1, 3)]
    near += [device(z, *at) for at in lines]
    near += [device(z, x, y, 1 - core)]
    near += [device((z + n) % 8, x, y, core) for n in (1, 2, 6, 7)]
    for other in near:
        pl.semaphore_signal(barrier, inc=1, device_id=other, device_id_type=MESH)

    loads[1].wait()
    own = spread(av_ref[...].astype(F32))
    counts[0] = own
    for g in range(4):
        for start in (80, 208):
            w[g, pl.ds(start, 48), :] = jnp.zeros((48, 1024), BF16)
    loads[0].wait()
    part = [x_ref[:, 0, pl.ds(512 * n, 512)] for n in range(5)]
    part.append(jnp.concatenate([x_ref[:, 0, pl.ds(2560, 440)], jnp.zeros((ROWS, 72), F32)], axis=1))
    d04 = part[0] - part[4]
    d13, s13 = part[1] - part[3], part[1] + part[3]
    split_rows(w, 0, 0, d04 + (d13 - part[5]) * HALF)
    split_rows(w, 0, 1, (part[5] - s13) * HALF - part[2])
    split_rows(w, 1, 0, part[0] + part[4] - part[2])
    split_rows(w, 1, 1, part[3] - part[1] - part[5])
    split_rows(w, 2, 0, d04 + (part[5] - d13) * HALF)
    split_rows(w, 2, 1, (part[5] - s13) * HALF + part[2])
    even, odd = part[0] + part[2] + part[4], s13 + part[5]
    split_rows(w, 3, 0, even + odd)
    split_rows(w, 3, 1, even - odd)

    pl.semaphore_wait(barrier, 11)
    count_copy = pltpu.make_async_remote_copy(
        src_ref=counts.at[0], dst_ref=counts.at[1], send_sem=count_sem.at[0], recv_sem=count_sem.at[1],
        device_id=device(z, x, (y + 2) % 4, core), device_id_type=MESH,
    )
    count_copy.start()
    for at in lines:
        pl.semaphore_signal(line_sem, inc=1, device_id=device(z, *at), device_id_type=MESH)

    power = jnp.zeros((32, 8, 128), F32)
    loads[2].wait()
    loads[3].wait()
    for g in range(4):
        if g == 2:
            pl.semaphore_wait(line_sem, 3)
            pl.semaphore_signal(core_sem, inc=1, device_id=device(z, x, y, 1 - core), device_id_type=MESH)
        high = lax.dot_general(table_ref[256 * g : 256 * (g + 1)], w[g], NT, preferred_element_type=F32)
        low = lax.dot_general(table_ref[1024 + 256 * g : 1280 + 256 * g], w[g], NT, preferred_element_type=F32)
        both = high + low
        value = (both[:, :128] + both[:, 128:]).reshape(32, 8, 128)
        xs[:, pl.ds(8 * g, 8), :] = value
        power = power + value * value
    power = jnp.sum(power.reshape(16, 16, 128), axis=1)
    triple = power + pltpu.roll(power, 127, 1) + pltpu.roll(power, 126, 1)
    phase = lax.broadcasted_iota(jnp.int32, (16, 128), 1) % 3
    total = jnp.where(phase == 0, triple, jnp.where(phase == 1, pltpu.roll(triple, 1, 1), pltpu.roll(triple, 2, 1)))
    amplitude = jnp.sqrt(total * (1.0 / 96) + 1e-06)
    count_copy.wait()
    count = (jnp.sum(own, axis=1, keepdims=True) + jnp.sum(counts[1], axis=1, keepdims=True)) * (1.0 / 3)
    weight = own / jnp.sqrt(jnp.round(count))
    factor = weight[0:1] / amplitude
    white[...] = (xs[...].reshape(16, 64, 128) * factor[:, None, :]).reshape(32, 32, 128).astype(BF16)

    pl.semaphore_wait(core_sem, 1)

    for px, py, pc in others:
        target = (px * 4 + py % 2 * 2 + pc) * 2 + py // 2
        pltpu.make_async_remote_copy(
            src_ref=white.at[target], dst_ref=rin.at[slot], send_sem=in_sem.at[0], recv_sem=in_sem.at[1],
            device_id=device(z, px, py, pc), device_id_type=MESH,
        ).start()
    pltpu.make_async_copy(rin.at[pl.ds(0, 31)], rin.at[pl.ds(0, 31)], in_sem.at[1]).wait()
    rin[slot] = white[slot]

    def swap(source, carry):
        start = source % 2 * 512 + source // 2
        turn[pl.ds(start, 32, stride=16), :] = rin[source].astype(F32)
        return carry

    lax.fori_loop(0, 32, swap, 0)
    loads[4].wait()
    pieces = turn[...].reshape(2, 16, 2, 16, 128)
    rows = jnp.concatenate(
        [pieces[s, :, part].reshape(256, 128).astype(BF16) for s in range(2) for part in range(2)], axis=1
    )
    plain = jnp.dot(rows, table_ref[4096:, :384], preferred_element_type=F32).astype(BF16)
    for c in range(3):
        gathered[c, z] = plain[:, 128 * c : 128 * (c + 1)].reshape(16, 16, 128)

    def moves(u, reach, come):
        size = 16 // HALVES
        signs = (1, -1) if reach < 4 else (1 - 2 * core,)
        for way, sign in enumerate(signs):
            piece = gathered.at[u // HALVES, (z + 8 - sign * come) % 8, pl.ds(u % HALVES * size, size)]
            yield pltpu.make_async_remote_copy(
                src_ref=piece, dst_ref=piece,
                send_sem=ring_send.at[u, reach - 1, way], recv_sem=ring_recv.at[u, reach - 1, way],
                device_id=device((z + 8 + sign * (reach - come)) % 8, x, y, core), device_id_type=MESH,
            )

    def forward(u, reach, come):
        for copy in moves(u, reach, come):
            copy.start()

    def arrive(u, reach):
        for copy in moves(u, reach, 0):
            copy.wait_recv()

    def own_side():
        turned = jnp.dot(rows, table_ref[4096:, 512:896], preferred_element_type=F32).astype(BF16)
        for c in range(3):
            left[:, pl.ds(16 * c, 16), :] = plain[:, 128 * c : 128 * (c + 1)].reshape(16, 16, 128)
            left[:, pl.ds(48 + 16 * c, 16), :] = turned[:, 128 * c : 128 * (c + 1)].reshape(16, 16, 128)

    lane = lax.broadcasted_iota(jnp.int32, (16, 128), 1) < 64

    def cross(b):
        for f in range(16):
            right = gathered[b, :, f].reshape(128, 128)
            product = lax.dot_general(left[f], right, NT, preferred_element_type=F32)
            for a in range(3):
                re = product[16 * a : 16 * (a + 1)]
                im = product[48 + 16 * a : 48 + 16 * (a + 1)]
                mixed = pltpu.roll(jnp.where(lane, im, re), 64, 1)
                stage[pl.ds(512 * a + f, 16, stride=16), :] = jnp.where(lane, re, mixed)
                stage[pl.ds(512 * a + 256 + f, 16, stride=16), :] = jnp.where(lane, mixed, im)
        send[b] = jnp.stack([stage[pl.ds(512 * a, 512), :].reshape(2, 16, 16, 128).astype(BF16) for a in range(3)], axis=2)

    def keep(b):
        target = stacks.at[b, slot] if b < 2 else last_ref.at[slot]
        return pltpu.make_async_copy(send.at[b, seg, slot // 2], target, own_sem.at[b])

    def ship(b, quarter):
        for px, py, pc in others[8 * quarter : 8 * quarter + 8]:
            pltpu.make_async_remote_copy(
                src_ref=send.at[b, py // 2, px * 4 + py % 2 * 2 + pc], dst_ref=stacks.at[b, slot] if b < 2 else last_ref.at[slot],
                send_sem=out_sem.at[b, 0], recv_sem=out_sem.at[b, 1],
                device_id=device(z, px, py, pc), device_id_type=MESH,
            ).start()
        if quarter == 3:
            keep(b).start()

    steps = {"F": forward, "A": arrive, "L": own_side, "C": cross, "S": ship}
    for step in SCHEDULE:
        steps[step[0]](*(int(digit) for digit in step[1:]))

    loads[5].wait()
    for b in range(2):
        keep(b).wait()
        whole = stacks.at[b, pl.ds(0, 31)]
        pltpu.make_async_copy(whole, whole, out_sem.at[b, 1]).wait()
        rows = lag_rows([stacks[b, :, a].reshape(512, 128) for a in range(3)])
        for n in range(4):
            half = table_ref[2048 + 1024 * (n // 2) : 3072 + 1024 * (n // 2), 512 * (n % 2) : 512 * (n % 2 + 1)]
            lagged = jnp.dot(rows, half, preferred_element_type=F32)
            lags[b, :, :, pl.ds(512 * n, 512)] = lagged.astype(BF16).reshape(3, 64, 512)

    pltpu.make_async_copy(white.at[pl.ds(0, 31)], white.at[pl.ds(0, 31)], in_sem.at[0]).wait()
    for u in range(3 * HALVES):
        for reach in range(1, 5):
            for copy in moves(u, reach, 0):
                copy.wait_send()
    keep(2).wait()
    whole = last_ref.at[pl.ds(0, 31)]
    pltpu.make_async_copy(whole, whole, out_sem.at[2, 1]).wait()
    for b in range(3):
        pltpu.make_async_copy(whole, whole, out_sem.at[b, 0]).wait()


def in_hbm(array):
    return pltpu.with_memory_space_constraint(array, pltpu.HBM)


def stacked(records, availability, tables):
    vmem, hbm = pl.BlockSpec(memory_space=pltpu.VMEM), pl.BlockSpec(memory_space=pl.ANY)
    return pl.pallas_call(
        stack_kernel,
        name="stack",
        out_shape=(
            pltpu.VMEM((32, 3, 16, 128), BF16),
            pltpu.VMEM((2, 3, 64, 2 * LAG), BF16),
        ),
        in_specs=[hbm, hbm, hbm],
        out_specs=(vmem, vmem),
        scratch_shapes=[
            pltpu.VMEM(records.shape, F32),
            pltpu.VMEM(availability.shape, jnp.int32),
            pltpu.VMEM(tables.shape, BF16),
            pltpu.VMEM((2, 32, 3, 16, 128), BF16),
            pltpu.VMEM((4, 256, 1024), BF16),
            pltpu.VMEM((32, 32, 128), F32),
            pltpu.VMEM((32, 32, 128), BF16),
            pltpu.VMEM((32, 32, 128), BF16),
            pltpu.VMEM((1024, 128), F32),
            pltpu.VMEM((3, 8, 16, 16, 128), BF16),
            pltpu.VMEM((16, 96, 128), BF16),
            pltpu.VMEM((1536, 128), F32),
            pltpu.VMEM((3, 2, 16, 3, 16, 128), BF16),
            pltpu.VMEM((2, 8, 128), F32),
            pltpu.SemaphoreType.DMA((6,)),
            pltpu.SemaphoreType.REGULAR,
            pltpu.SemaphoreType.REGULAR,
            pltpu.SemaphoreType.DMA((2,)),
            pltpu.SemaphoreType.DMA((2,)),
            pltpu.SemaphoreType.DMA((3 * HALVES, 4, 2)),
            pltpu.SemaphoreType.DMA((3 * HALVES, 4, 2)),
            pltpu.SemaphoreType.DMA((3, 2)),
            pltpu.SemaphoreType.DMA((3,)),
        ],
        compiler_params=pltpu.CompilerParams(
            collective_id=0, has_side_effects=True, vmem_limit_bytes=40 << 20
        ),
    )(in_hbm(records), in_hbm(availability), in_hbm(tables))


def lag_kernel(last_ref, part_ref, table_ref, out_hbm, lags, part_sem, out_sem):
    copies = [
        pltpu.make_async_copy(part_ref.at[b, a], out_hbm.at[3 * a + b], part_sem.at[b, a])
        for b in range(2)
        for a in range(3)
    ]
    for copy in copies:
        copy.start()
    rows = lag_rows([last_ref[:, a].reshape(512, 128) for a in range(3)])
    for n in range(4):
        column = pl.ds(512 * n, 512)
        lagged = jnp.dot(rows, table_ref[:, column], preferred_element_type=F32)
        lags[:, :, column] = lagged.astype(BF16).reshape(3, 64, 512)
        for a in range(3):
            copies.append(
                pltpu.make_async_copy(
                    lags.at[a, :, column], out_hbm.at[3 * a + 2, :, column], out_sem.at[n, a]
                )
            )
            copies[-1].start()
    for copy in copies:
        copy.wait()


def to_lags(last, part, table):
    vmem = pl.BlockSpec(memory_space=pltpu.VMEM)
    return pl.pallas_call(
        lag_kernel,
        name="lags",
        out_shape=jax.ShapeDtypeStruct((9, 64, 2 * LAG), BF16),
        in_specs=[vmem] * 3,
        out_specs=pl.BlockSpec(memory_space=pl.ANY),
        scratch_shapes=[
            pltpu.VMEM((3, 64, 2 * LAG), BF16),
            pltpu.SemaphoreType.DMA((2, 3)),
            pltpu.SemaphoreType.DMA((4, 3)),
        ],
        compiler_params=pltpu.CompilerParams(vmem_limit_bytes=40 << 20),
    )(*(pltpu.with_memory_space_constraint(array, pltpu.VMEM) for array in (last, part, table)))


def body(records, availability):
    samples = records.shape[-1]
    inverse = inverse_table()
    last, part = stacked(records.reshape(ROWS, 1, samples), availability, jnp.asarray(all_tables(inverse)))
    lagged = to_lags(last, part, jnp.asarray(inverse))
    return jnp.transpose(lagged, (1, 0, 2))[None]


def solution(mesh):
    placed = (P("blk", "seg", None, None), P("blk", "seg"))
    return jax.shard_map(
        body, mesh=mesh, in_specs=placed, out_specs=P("blk", "seg", None, None), check_vma=False
    )
```

```python
import functools
import math

import jax
import jax.numpy as jnp
import ml_dtypes
import numpy as np
from jax import lax
from jax.experimental import pallas as pl
from jax.experimental.pallas import tpu as pltpu
from jax.sharding import PartitionSpec as P

MESH = pl.DeviceIdType.MESH
F32 = jnp.float32
BF16 = jnp.bfloat16
NFFT = 4096
FREQS = 512
LAG = 1024
SEGS = 30
ROWS = 96
RESIDUES = ((1, 7), (2, 6), (3, 5), (8, 4))
HALF = math.sqrt(0.5)
UNITS = ((0, 0, 8), (0, 8, 8), (1, 0, 16), (2, 0, 16))
OTHERS = sorted(
    ((dx, dy, dc) for dx in range(4) for dy in range(4) for dc in range(2) if dx or dy or dc),
    key=lambda d: (-min(d[0], 4 - d[0]) - min(d[1], 4 - d[1]), (5 * d[0] + 3 * d[1] + d[2]) % 7),
)
SCHEDULE = (
    ["P0", "F010", "P1", "F110", "F210", "L", "A01", "F021", "A11", "F121", "F310", "A21", "F221"]
    + ["A02", "F032", "F042", "A12", "F132", "F142", "A31", "F321", "A22", "F232", "F242"]
    + ["A03", "A13", "A04", "A14", "C0", "S00", "S01", "A32", "F332", "F342", "S02", "S03"]
    + ["A23", "A24", "C1", "S10", "S11", "S12", "S13"]
    + ["A33", "A34", "C2", "S20", "S21", "S22", "S23"]
)
NT = (((1,), (1,)), ((), ()))


def bin_of(p, f):
    return 16 * p + 8 * (f % 2) + np.array(RESIDUES)[f // 4, f // 2 % 2]


def forward_table():
    table = np.zeros((4, 32, 2, 2, 2, 2, 512))
    n = np.arange(512)
    for g in range(4):
        for which in range(2):
            for odd in range(2):
                k = 16 * np.arange(32) + 8 * odd + RESIDUES[g][which]
                angle = (k[:, None] * n[None, :] % NFFT) * (2 * np.pi / NFFT)
                cos, sin = np.cos(angle), np.sin(angle)
                if g == 3:
                    table[g, :, which, odd, 0, which] = cos
                    table[g, :, which, odd, 1, which] = -sin
                else:
                    sign = 1 - 2 * which
                    table[g, :, which, odd, 0, 0] = cos
                    table[g, :, which, odd, 0, 1] = sign * sin
                    table[g, :, which, odd, 1, 0] = -sin
                    table[g, :, which, odd, 1, 1] = sign * cos
    table = table.reshape(4, 256, 1024)
    high = table.astype(ml_dtypes.bfloat16)
    low = (table - high.astype(np.float64)).astype(ml_dtypes.bfloat16)
    return high.reshape(1024, 1024), low.reshape(1024, 1024)


def inverse_table():
    p, f = np.meshgrid(np.arange(32), np.arange(16), indexing="ij")
    k = bin_of(p, f).reshape(-1)
    tau = np.arange(2 * LAG) - LAG
    angle = (k[:, None] * tau[None, :] % NFFT) * (2 * np.pi / NFFT)
    table = np.concatenate([np.cos(angle), -np.sin(angle)], axis=0) * (2.0 / NFFT)
    return table.astype(ml_dtypes.bfloat16)


def place_table():
    plain = np.zeros((2, 2, 128, 4, 128))
    turned = np.zeros((2, 2, 128, 4, 128))
    for seg in range(2):
        for s in range(SEGS):
            for c in range(3):
                for part in range(2):
                    plain[seg, part, 3 * s + c, c, 64 * part + 30 * seg + s] = 1
                turned[seg, 1, 3 * s + c, c, 30 * seg + s] = 1
                turned[seg, 0, 3 * s + c, c, 64 + 30 * seg + s] = -1
    both = np.concatenate([plain.reshape(512, 512), turned.reshape(512, 512)], axis=1)
    return both.astype(ml_dtypes.bfloat16)


def all_tables(inverse):
    return np.concatenate([*forward_table(), inverse[:, :LAG], inverse[:, LAG:], place_table()], axis=0)


def place():
    blk, seg = lax.axis_index("blk"), lax.axis_index("seg")
    z, rest = blk // 16, blk % 16
    return z, rest // 4, seg * 2 + rest // 2 % 2, rest % 2, seg


def device(z, x, y, core):
    return (z * 16 + x * 4 + y % 2 * 2 + core, y // 2)


def lag_rows(blocks):
    turned = [block.T for block in blocks]
    return jnp.concatenate([jnp.concatenate([one[:64], one[64:]], axis=1) for one in turned], axis=0)


def spread(av):
    column = lax.broadcasted_iota(jnp.int32, (SEGS, 128), 1)
    row = lax.broadcasted_iota(jnp.int32, (SEGS, 128), 0)
    pick = ((column >= 3 * row) & (column < 3 * row + 3)).astype(F32)
    return jnp.dot(jnp.broadcast_to(av, (8, SEGS)), pick, preferred_element_type=F32)


def split_rows(w_ref, g, half, value):
    high = value.astype(BF16)
    low = (value - high.astype(F32)).astype(BF16)
    columns = pl.ds(512 * half, 512)
    w_ref[g, pl.ds(0, ROWS), columns] = high
    w_ref[g, pl.ds(128, ROWS), columns] = low


def stack_kernel(
    x_hbm, av_hbm, table_hbm, last_ref, lags,
    x_ref, av_ref, table_ref, stacks,
    w, xs, white, rin, turn, gathered, left, stage, send, counts,
    load_sem, line_sem, core_sem, count_sem, in_sem, ring_send, ring_recv, out_sem, own_sem,
):
    z, x, y, core, seg = place()
    slot = (x * 4 + y % 2 * 2 + core) * 2 + seg
    others = [((x + dx) % 4, (y + dy) % 4, (core + dc) % 2) for dx, dy, dc in OTHERS]
    parts = [pl.ds(first, rows) for first, rows in ((0, 1024), (1024, 1024), (4096, 512), (2048, 2048))]
    loads = [pltpu.make_async_copy(x_hbm, x_ref.at[pl.ds(0, 90)], load_sem.at[4]), pltpu.make_async_copy(av_hbm, av_ref, load_sem.at[5])]
    loads += [
        pltpu.make_async_copy(table_hbm.at[rows], table_ref.at[rows], load_sem.at[n]) for n, rows in enumerate(parts)
    ]
    for load in loads:
        load.start()

    barrier = pltpu.get_barrier_semaphore()

    lines = [((x + n) % 4, y, core) for n in range(1, 4)]
    near = [device(z, x, (y + n) % 4, core) for n in (2, 1, 3)]
    near += [device(z, *at) for at in lines]
    near += [device(z, x, y, 1 - core)]
    near += [device((z + n) % 8, x, y, core) for n in (1, 2, 6, 7)]
    for other in near:
        pl.semaphore_signal(barrier, inc=1, device_id=other, device_id_type=MESH)

    loads[1].wait()
    own = spread(av_ref[...].astype(F32))
    counts[0] = own
    for g in range(4):
        for start in (ROWS, 128 + ROWS):
            w[g, pl.ds(start, 32), :] = jnp.zeros((32, 1024), BF16)
    x_ref[pl.ds(90, ROWS - 90)] = jnp.zeros((ROWS - 90, 1, x_ref.shape[2]), F32)
    loads[0].wait()
    part = [x_ref[:, 0, pl.ds(512 * n, 512)] for n in range(5)]
    part.append(jnp.concatenate([x_ref[:, 0, pl.ds(2560, 440)], jnp.zeros((ROWS, 72), F32)], axis=1))
    d04 = part[0] - part[4]
    d13, s13 = part[1] - part[3], part[1] + part[3]
    split_rows(w, 0, 0, d04 + (d13 - part[5]) * HALF)
    split_rows(w, 0, 1, (part[5] - s13) * HALF - part[2])
    split_rows(w, 1, 0, part[0] + part[4] - part[2])
    split_rows(w, 1, 1, part[3] - part[1] - part[5])
    split_rows(w, 2, 0, d04 + (part[5] - d13) * HALF)
    split_rows(w, 2, 1, (part[5] - s13) * HALF + part[2])
    even, odd = part[0] + part[2] + part[4], s13 + part[5]
    split_rows(w, 3, 0, even + odd)
    split_rows(w, 3, 1, even - odd)

    pl.semaphore_wait(barrier, 11)
    count_copy = pltpu.make_async_remote_copy(
        src_ref=counts.at[0], dst_ref=counts.at[1], send_sem=count_sem.at[0], recv_sem=count_sem.at[1],
        device_id=device(z, x, (y + 2) % 4, core), device_id_type=MESH,
    )
    count_copy.start()
    for at in lines:
        pl.semaphore_signal(line_sem, inc=1, device_id=device(z, *at), device_id_type=MESH)

    power = jnp.zeros((32, 8, 128), F32)
    loads[2].wait()
    loads[3].wait()
    for g in range(4):
        if g == 2:
            pl.semaphore_wait(line_sem, 3)
            pl.semaphore_signal(core_sem, inc=1, device_id=device(z, x, y, 1 - core), device_id_type=MESH)
        high = lax.dot_general(table_ref[256 * g : 256 * (g + 1)], w[g], NT, preferred_element_type=F32)
        low = lax.dot_general(table_ref[1024 + 256 * g : 1280 + 256 * g], w[g], NT, preferred_element_type=F32)
        both = high + low
        value = (both[:, :128] + both[:, 128:]).reshape(32, 8, 128)
        xs[:, pl.ds(8 * g, 8), :] = value
        power = power + value * value
    power = jnp.sum(power.reshape(16, 16, 128), axis=1)
    triple = power + pltpu.roll(power, 127, 1) + pltpu.roll(power, 126, 1)
    phase = lax.broadcasted_iota(jnp.int32, (16, 128), 1) % 3
    total = jnp.where(phase == 0, triple, jnp.where(phase == 1, pltpu.roll(triple, 1, 1), pltpu.roll(triple, 2, 1)))
    amplitude = jnp.sqrt(total * (1.0 / 96) + 1e-06)
    count_copy.wait()
    count = (jnp.sum(own, axis=1, keepdims=True) + jnp.sum(counts[1], axis=1, keepdims=True)) * (1.0 / 3)
    weight = own / jnp.sqrt(jnp.round(count))
    factor = weight[0:1] / amplitude
    white[...] = (xs[...].reshape(16, 64, 128) * factor[:, None, :]).reshape(32, 32, 128).astype(BF16)

    pl.semaphore_wait(core_sem, 1)

    for px, py, pc in others:
        target = (px * 4 + py % 2 * 2 + pc) * 2 + py // 2
        pltpu.make_async_remote_copy(
            src_ref=white.at[target], dst_ref=rin.at[slot], send_sem=in_sem.at[0], recv_sem=in_sem.at[1],
            device_id=device(z, px, py, pc), device_id_type=MESH,
        ).start()
    pltpu.make_async_copy(rin.at[pl.ds(0, 31)], rin.at[pl.ds(0, 31)], in_sem.at[1]).wait()
    rin[slot] = white[slot]

    def swap(source, carry):
        start = source % 2 * 512 + source // 2
        turn[pl.ds(start, 32, stride=16), :] = rin[source].astype(F32)
        return carry

    lax.fori_loop(0, 32, swap, 0)
    loads[4].wait()
    pieces = turn[...].reshape(2, 16, 2, 16, 128)
    rows = jnp.concatenate(
        [pieces[s, :, part].reshape(256, 128).astype(BF16) for s in range(2) for part in range(2)], axis=1
    )
    def own_units(half):
        plain = jnp.dot(rows[128 * half : 128 * half + 128], table_ref[4096:, :384], preferred_element_type=F32)
        plain = plain.astype(BF16)
        for c in range(3):
            gathered[c, z, pl.ds(8 * half, 8)] = plain[:, 128 * c : 128 * (c + 1)].reshape(8, 16, 128)

    def moves(u, reach, come):
        c, first, bins = UNITS[u]
        signs = (1, -1) if reach < 4 else (1 - 2 * core,)
        for way, sign in enumerate(signs):
            piece = gathered.at[c, (z + 8 - sign * come) % 8, pl.ds(first, bins)]
            yield pltpu.make_async_remote_copy(
                src_ref=piece, dst_ref=piece,
                send_sem=ring_send.at[u, reach - 1, way], recv_sem=ring_recv.at[u, reach - 1, way],
                device_id=device((z + 8 + sign * (reach - come)) % 8, x, y, core), device_id_type=MESH,
            )

    def forward(u, reach, come):
        for copy in moves(u, reach, come):
            copy.start()

    def arrive(u, reach):
        for copy in moves(u, reach, 0):
            copy.wait_recv()

    def own_side():
        turned = jnp.dot(rows, table_ref[4096:, 512:896], preferred_element_type=F32).astype(BF16)
        for c in range(3):
            left[:, pl.ds(16 * c, 16), :] = gathered[c, z]
            left[:, pl.ds(48 + 16 * c, 16), :] = turned[:, 128 * c : 128 * (c + 1)].reshape(16, 16, 128)

    lane = lax.broadcasted_iota(jnp.int32, (16, 128), 1) < 64

    def cross(b):
        for f in range(16):
            right = gathered[b, :, f].reshape(128, 128)
            product = lax.dot_general(left[f], right, NT, preferred_element_type=F32)
            for a in range(3):
                re = product[16 * a : 16 * (a + 1)]
                im = product[48 + 16 * a : 48 + 16 * (a + 1)]
                mixed = pltpu.roll(jnp.where(lane, im, re), 64, 1)
                stage[pl.ds(512 * a + f, 16, stride=16), :] = jnp.where(lane, re, mixed)
                stage[pl.ds(512 * a + 256 + f, 16, stride=16), :] = jnp.where(lane, mixed, im)
        send[b] = jnp.stack([stage[pl.ds(512 * a, 512), :].reshape(2, 16, 16, 128).astype(BF16) for a in range(3)], axis=2)

    def keep(b):
        target = stacks.at[b, slot] if b < 2 else last_ref.at[slot]
        return pltpu.make_async_copy(send.at[b, seg, slot // 2], target, own_sem.at[b])

    def ship(b, quarter):
        for px, py, pc in others[8 * quarter : 8 * quarter + 8]:
            pltpu.make_async_remote_copy(
                src_ref=send.at[b, py // 2, px * 4 + py % 2 * 2 + pc], dst_ref=stacks.at[b, slot] if b < 2 else last_ref.at[slot],
                send_sem=out_sem.at[b, 0], recv_sem=out_sem.at[b, 1],
                device_id=device(z, px, py, pc), device_id_type=MESH,
            ).start()
        if quarter == 3:
            keep(b).start()

    steps = {"F": forward, "A": arrive, "P": own_units, "L": own_side, "C": cross, "S": ship}
    for step in SCHEDULE:
        steps[step[0]](*(int(digit) for digit in step[1:]))

    loads[5].wait()
    for b in range(2):
        keep(b).wait()
        whole = stacks.at[b, pl.ds(0, 31)]
        pltpu.make_async_copy(whole, whole, out_sem.at[b, 1]).wait()
        rows = lag_rows([stacks[b, :, a].reshape(512, 128) for a in range(3)])
        for n in range(4):
            half = table_ref[2048 + 1024 * (n // 2) : 3072 + 1024 * (n // 2), 512 * (n % 2) : 512 * (n % 2 + 1)]
            lagged = jnp.dot(rows, half, preferred_element_type=F32)
            lags[b, :, :, pl.ds(512 * n, 512)] = lagged.astype(BF16).reshape(3, 64, 512)

    pltpu.make_async_copy(white.at[pl.ds(0, 31)], white.at[pl.ds(0, 31)], in_sem.at[0]).wait()
    for u in range(len(UNITS)):
        for reach in range(1, 5):
            for copy in moves(u, reach, 0):
                copy.wait_send()
    keep(2).wait()
    whole = last_ref.at[pl.ds(0, 31)]
    pltpu.make_async_copy(whole, whole, out_sem.at[2, 1]).wait()
    for b in range(3):
        pltpu.make_async_copy(whole, whole, out_sem.at[b, 0]).wait()


def in_hbm(array):
    return pltpu.with_memory_space_constraint(array, pltpu.HBM)


def stacked(records, availability, tables):
    vmem, hbm = pl.BlockSpec(memory_space=pltpu.VMEM), pl.BlockSpec(memory_space=pl.ANY)
    return pl.pallas_call(
        stack_kernel,
        name="stack",
        out_shape=(
            pltpu.VMEM((32, 3, 16, 128), BF16),
            pltpu.VMEM((2, 3, 64, 2 * LAG), BF16),
        ),
        in_specs=[hbm, hbm, hbm],
        out_specs=(vmem, vmem),
        scratch_shapes=[
            pltpu.VMEM((ROWS, 1, records.shape[2]), F32),
            pltpu.VMEM(availability.shape, jnp.int32),
            pltpu.VMEM(tables.shape, BF16),
            pltpu.VMEM((2, 32, 3, 16, 128), BF16),
            pltpu.VMEM((4, 256, 1024), BF16),
            pltpu.VMEM((32, 32, 128), F32),
            pltpu.VMEM((32, 32, 128), BF16),
            pltpu.VMEM((32, 32, 128), BF16),
            pltpu.VMEM((1024, 128), F32),
            pltpu.VMEM((3, 8, 16, 16, 128), BF16),
            pltpu.VMEM((16, 96, 128), BF16),
            pltpu.VMEM((1536, 128), F32),
            pltpu.VMEM((3, 2, 16, 3, 16, 128), BF16),
            pltpu.VMEM((2, 8, 128), F32),
            pltpu.SemaphoreType.DMA((6,)),
            pltpu.SemaphoreType.REGULAR,
            pltpu.SemaphoreType.REGULAR,
            pltpu.SemaphoreType.DMA((2,)),
            pltpu.SemaphoreType.DMA((2,)),
            pltpu.SemaphoreType.DMA((len(UNITS), 4, 2)),
            pltpu.SemaphoreType.DMA((len(UNITS), 4, 2)),
            pltpu.SemaphoreType.DMA((3, 2)),
            pltpu.SemaphoreType.DMA((3,)),
        ],
        compiler_params=pltpu.CompilerParams(
            collective_id=0, has_side_effects=True, vmem_limit_bytes=40 << 20
        ),
    )(in_hbm(records), in_hbm(availability), in_hbm(tables))


def lag_kernel(last_ref, part_ref, table_ref, out_hbm, lags, part_sem, out_sem):
    copies = [
        pltpu.make_async_copy(part_ref.at[b, a], out_hbm.at[3 * a + b], part_sem.at[b, a])
        for b in range(2)
        for a in range(3)
    ]
    for copy in copies:
        copy.start()
    rows = lag_rows([last_ref[:, a].reshape(512, 128) for a in range(3)])
    for n in range(4):
        column = pl.ds(512 * n, 512)
        lagged = jnp.dot(rows, table_ref[:, column], preferred_element_type=F32)
        lags[:, :, column] = lagged.astype(BF16).reshape(3, 64, 512)
        for a in range(3):
            copies.append(
                pltpu.make_async_copy(
                    lags.at[a, :, column], out_hbm.at[3 * a + 2, :, column], out_sem.at[n, a]
                )
            )
            copies[-1].start()
    for copy in copies:
        copy.wait()


def to_lags(last, part, table):
    vmem = pl.BlockSpec(memory_space=pltpu.VMEM)
    return pl.pallas_call(
        lag_kernel,
        name="lags",
        out_shape=jax.ShapeDtypeStruct((9, 64, 2 * LAG), BF16),
        in_specs=[vmem] * 3,
        out_specs=pl.BlockSpec(memory_space=pl.ANY),
        scratch_shapes=[
            pltpu.VMEM((3, 64, 2 * LAG), BF16),
            pltpu.SemaphoreType.DMA((2, 3)),
            pltpu.SemaphoreType.DMA((4, 3)),
        ],
        compiler_params=pltpu.CompilerParams(vmem_limit_bytes=40 << 20),
    )(*(pltpu.with_memory_space_constraint(array, pltpu.VMEM) for array in (last, part, table)))


def body(records, availability):
    samples = records.shape[-1]
    inverse = inverse_table()
    last, part = stacked(records.reshape(90, 1, samples), availability, jnp.asarray(all_tables(inverse)))
    lagged = to_lags(last, part, jnp.asarray(inverse))
    return jnp.transpose(lagged, (1, 0, 2))[None]


def solution(mesh):
    placed = (P("blk", "seg", None, None), P("blk", "seg"))
    return jax.shard_map(
        body, mesh=mesh, in_specs=placed, out_specs=P("blk", "seg", None, None), check_vma=False
    )
```

```python
import functools
import math

import jax
import jax.numpy as jnp
import ml_dtypes
import numpy as np
from jax import lax
from jax.experimental import pallas as pl
from jax.experimental.pallas import tpu as pltpu
from jax.sharding import PartitionSpec as P

MESH = pl.DeviceIdType.MESH
F32 = jnp.float32
BF16 = jnp.bfloat16
NFFT = 4096
FREQS = 512
LAG = 1024
SEGS = 30
ROWS = 96
RESIDUES = ((1, 7), (2, 6), (3, 5), (8, 4))
HALF = math.sqrt(0.5)
UNITS = ((0, 0, 8), (0, 8, 8), (1, 0, 16), (2, 0, 16))
OTHERS = sorted(
    ((dx, dy, dc) for dx in range(4) for dy in range(4) for dc in range(2) if dx or dy or dc),
    key=lambda d: (-min(d[0], 4 - d[0]) - min(d[1], 4 - d[1]), (5 * d[0] + 3 * d[1] + d[2]) % 7),
)
SCHEDULE = (
    ["P0", "F010", "P1", "F110", "F210", "L", "A01", "F021", "A11", "F121", "F310", "A21", "F221"]
    + ["A02", "F032", "F042", "A12", "F132", "F142", "A31", "F321", "A22", "F232", "F242"]
    + ["A03", "A13", "A04", "A14", "C0", "S00", "S01", "A32", "F332", "F342", "S02", "S03"]
    + ["A23", "A24", "C1", "S10", "S11", "S12", "S13"]
    + ["A33", "A34", "C2", "S20", "S21", "S22", "S23"]
)
NT = (((1,), (1,)), ((), ()))


def bin_of(p, f):
    return 16 * p + 8 * (f % 2) + np.array(RESIDUES)[f // 4, f // 2 % 2]


def forward_table():
    table = np.zeros((4, 32, 2, 2, 2, 2, 512))
    n = np.arange(512)
    for g in range(4):
        for which in range(2):
            for odd in range(2):
                k = 16 * np.arange(32) + 8 * odd + RESIDUES[g][which]
                angle = (k[:, None] * n[None, :] % NFFT) * (2 * np.pi / NFFT)
                cos, sin = np.cos(angle), np.sin(angle)
                if g == 3:
                    table[g, :, which, odd, 0, which] = cos
                    table[g, :, which, odd, 1, which] = -sin
                else:
                    sign = 1 - 2 * which
                    table[g, :, which, odd, 0, 0] = cos
                    table[g, :, which, odd, 0, 1] = sign * sin
                    table[g, :, which, odd, 1, 0] = -sin
                    table[g, :, which, odd, 1, 1] = sign * cos
    table = table.reshape(4, 256, 1024)
    high = table.astype(ml_dtypes.bfloat16)
    low = (table - high.astype(np.float64)).astype(ml_dtypes.bfloat16)
    return high.reshape(1024, 1024), low.reshape(1024, 1024)


def inverse_table():
    p, f = np.meshgrid(np.arange(32), np.arange(16), indexing="ij")
    k = bin_of(p, f).reshape(-1)
    tau = np.arange(2 * LAG) - LAG
    angle = (k[:, None] * tau[None, :] % NFFT) * (2 * np.pi / NFFT)
    table = np.concatenate([np.cos(angle), -np.sin(angle)], axis=0) * (2.0 / NFFT)
    return table.astype(ml_dtypes.bfloat16)


def place_table():
    plain = np.zeros((2, 2, 128, 4, 128))
    turned = np.zeros((2, 2, 128, 4, 128))
    for seg in range(2):
        for s in range(SEGS):
            for c in range(3):
                for part in range(2):
                    plain[seg, part, 3 * s + c, c, 64 * part + 30 * seg + s] = 1
                turned[seg, 1, 3 * s + c, c, 30 * seg + s] = 1
                turned[seg, 0, 3 * s + c, c, 64 + 30 * seg + s] = -1
    both = np.concatenate([plain.reshape(512, 512), turned.reshape(512, 512)], axis=1)
    return both.astype(ml_dtypes.bfloat16)


def all_tables(inverse):
    return np.concatenate([*forward_table(), inverse[:, :LAG], inverse[:, LAG:], place_table()], axis=0)


def place():
    blk, seg = lax.axis_index("blk"), lax.axis_index("seg")
    z, rest = blk // 16, blk % 16
    return z, rest // 4, seg * 2 + rest // 2 % 2, rest % 2, seg


def device(z, x, y, core):
    return (z * 16 + x * 4 + y % 2 * 2 + core, y // 2)


def lag_rows(blocks):
    turned = [block.T for block in blocks]
    return jnp.concatenate([jnp.concatenate([one[:64], one[64:]], axis=1) for one in turned], axis=0)


def spread(av):
    column = lax.broadcasted_iota(jnp.int32, (SEGS, 128), 1)
    row = lax.broadcasted_iota(jnp.int32, (SEGS, 128), 0)
    pick = ((column >= 3 * row) & (column < 3 * row + 3)).astype(F32)
    return jnp.dot(jnp.broadcast_to(av, (8, SEGS)), pick, preferred_element_type=F32)


def split_rows(w_ref, g, half, value):
    high = value.astype(BF16)
    low = (value - high.astype(F32)).astype(BF16)
    columns = pl.ds(512 * half, 512)
    w_ref[g, pl.ds(0, ROWS), columns] = high
    w_ref[g, pl.ds(128, ROWS), columns] = low


def stack_kernel(
    x_hbm, av_hbm, table_hbm, last_ref, lags,
    x_ref, av_ref, table_ref, stacks,
    w, xs, white, rin, turn, gathered, left, stage, send, counts,
    load_sem, line_sem, core_sem, count_sem, in_sem, ring_send, ring_recv, out_sem, own_sem,
):
    z, x, y, core, seg = place()
    slot = (x * 4 + y % 2 * 2 + core) * 2 + seg
    others = [((x + dx) % 4, (y + dy) % 4, (core + dc) % 2) for dx, dy, dc in OTHERS]
    parts = [pl.ds(first, rows) for first, rows in ((0, 1024), (1024, 1024), (4096, 512), (2048, 2048))]
    loads = [pltpu.make_async_copy(x_hbm, x_ref.at[pl.ds(0, 90)], load_sem.at[4]), pltpu.make_async_copy(av_hbm, av_ref, load_sem.at[5])]
    loads += [
        pltpu.make_async_copy(table_hbm.at[rows], table_ref.at[rows], load_sem.at[n]) for n, rows in enumerate(parts)
    ]
    for load in loads:
        load.start()

    barrier = pltpu.get_barrier_semaphore()

    lines = [((x + n) % 4, y, core) for n in range(1, 4)]
    near = [device(z, x, (y + n) % 4, core) for n in (2, 1, 3)]
    near += [device(z, *at) for at in lines]
    near += [device(z, x, y, 1 - core)]
    near += [device((z + n) % 8, x, y, core) for n in (1, 2, 6, 7)]
    for other in near:
        pl.semaphore_signal(barrier, inc=1, device_id=other, device_id_type=MESH)

    loads[1].wait()
    own = spread(av_ref[...].astype(F32))
    counts[0] = own
    for g in range(4):
        for start in (ROWS, 128 + ROWS):
            w[g, pl.ds(start, 32), :] = jnp.zeros((32, 1024), BF16)
    x_ref[pl.ds(90, ROWS - 90)] = jnp.zeros((ROWS - 90, 1, x_ref.shape[2]), F32)
    loads[0].wait()
    part = [x_ref[:, 0, pl.ds(512 * n, 512)] for n in range(5)]
    part.append(jnp.concatenate([x_ref[:, 0, pl.ds(2560, 440)], jnp.zeros((ROWS, 72), F32)], axis=1))
    d04 = part[0] - part[4]
    d13, s13 = part[1] - part[3], part[1] + part[3]
    split_rows(w, 0, 0, d04 + (d13 - part[5]) * HALF)
    split_rows(w, 0, 1, (part[5] - s13) * HALF - part[2])
    split_rows(w, 1, 0, part[0] + part[4] - part[2])
    split_rows(w, 1, 1, part[3] - part[1] - part[5])
    split_rows(w, 2, 0, d04 + (part[5] - d13) * HALF)
    split_rows(w, 2, 1, (part[5] - s13) * HALF + part[2])
    even, odd = part[0] + part[2] + part[4], s13 + part[5]
    split_rows(w, 3, 0, even + odd)
    split_rows(w, 3, 1, even - odd)

    pl.semaphore_wait(barrier, 11)
    count_copy = pltpu.make_async_remote_copy(
        src_ref=counts.at[0], dst_ref=counts.at[1], send_sem=count_sem.at[0], recv_sem=count_sem.at[1],
        device_id=device(z, x, (y + 2) % 4, core), device_id_type=MESH,
    )
    count_copy.start()
    for at in lines:
        pl.semaphore_signal(line_sem, inc=1, device_id=device(z, *at), device_id_type=MESH)

    power = jnp.zeros((32, 8, 128), F32)
    loads[2].wait()
    loads[3].wait()
    for g in range(4):
        if g == 2:
            pl.semaphore_wait(line_sem, 3)
            pl.semaphore_signal(core_sem, inc=1, device_id=device(z, x, y, 1 - core), device_id_type=MESH)
        high = lax.dot_general(table_ref[256 * g : 256 * (g + 1)], w[g], NT, preferred_element_type=F32)
        low = lax.dot_general(table_ref[1024 + 256 * g : 1280 + 256 * g], w[g], NT, preferred_element_type=F32)
        both = high + low
        value = (both[:, :128] + both[:, 128:]).reshape(32, 8, 128)
        xs[:, pl.ds(8 * g, 8), :] = value
        power = power + value * value
    power = jnp.sum(power.reshape(16, 16, 128), axis=1)
    triple = power + pltpu.roll(power, 127, 1) + pltpu.roll(power, 126, 1)
    phase = lax.broadcasted_iota(jnp.int32, (16, 128), 1) % 3
    total = jnp.where(phase == 0, triple, jnp.where(phase == 1, pltpu.roll(triple, 1, 1), pltpu.roll(triple, 2, 1)))
    amplitude = jnp.sqrt(total * (1.0 / 96) + 1e-06)
    factor = own[0:1] / amplitude
    xs[...] = (xs[...].reshape(16, 64, 128) * factor[:, None, :]).reshape(32, 32, 128)
    count_copy.wait()
    count = (jnp.sum(own, axis=1, keepdims=True) + jnp.sum(counts[1], axis=1, keepdims=True)) * (1.0 / 3)
    scale = jnp.broadcast_to(1.0 / jnp.sqrt(jnp.round(count)), (8, 128))[0:1]
    white[...] = (xs[...] * scale[None]).astype(BF16)

    pl.semaphore_wait(core_sem, 1)

    for px, py, pc in others:
        target = (px * 4 + py % 2 * 2 + pc) * 2 + py // 2
        pltpu.make_async_remote_copy(
            src_ref=white.at[target], dst_ref=rin.at[slot], send_sem=in_sem.at[0], recv_sem=in_sem.at[1],
            device_id=device(z, px, py, pc), device_id_type=MESH,
        ).start()
    pltpu.make_async_copy(rin.at[pl.ds(0, 31)], rin.at[pl.ds(0, 31)], in_sem.at[1]).wait()
    rin[slot] = white[slot]

    def swap(source, carry):
        start = source % 2 * 512 + source // 2
        turn[pl.ds(start, 32, stride=16), :] = rin[source].astype(F32)
        return carry

    lax.fori_loop(0, 32, swap, 0)
    loads[4].wait()
    pieces = turn[...].reshape(2, 16, 2, 16, 128)
    rows = jnp.concatenate(
        [pieces[s, :, part].reshape(256, 128).astype(BF16) for s in range(2) for part in range(2)], axis=1
    )
    def own_units(half):
        plain = jnp.dot(rows[128 * half : 128 * half + 128], table_ref[4096:, :384], preferred_element_type=F32)
        plain = plain.astype(BF16)
        for c in range(3):
            gathered[c, z, pl.ds(8 * half, 8)] = plain[:, 128 * c : 128 * (c + 1)].reshape(8, 16, 128)

    def moves(u, reach, come):
        c, first, bins = UNITS[u]
        signs = (1, -1) if reach < 4 else (1 - 2 * core,)
        for way, sign in enumerate(signs):
            piece = gathered.at[c, (z + 8 - sign * come) % 8, pl.ds(first, bins)]
            yield pltpu.make_async_remote_copy(
                src_ref=piece, dst_ref=piece,
                send_sem=ring_send.at[u, reach - 1, way], recv_sem=ring_recv.at[u, reach - 1, way],
                device_id=device((z + 8 + sign * (reach - come)) % 8, x, y, core), device_id_type=MESH,
            )

    def forward(u, reach, come):
        for copy in moves(u, reach, come):
            copy.start()

    def arrive(u, reach):
        for copy in moves(u, reach, 0):
            copy.wait_recv()

    def own_side():
        turned = jnp.dot(rows, table_ref[4096:, 512:896], preferred_element_type=F32).astype(BF16)
        for c in range(3):
            left[:, pl.ds(16 * c, 16), :] = gathered[c, z]
            left[:, pl.ds(48 + 16 * c, 16), :] = turned[:, 128 * c : 128 * (c + 1)].reshape(16, 16, 128)

    lane = lax.broadcasted_iota(jnp.int32, (16, 128), 1) < 64

    def cross(b):
        for f in range(16):
            right = gathered[b, :, f].reshape(128, 128)
            product = lax.dot_general(left[f], right, NT, preferred_element_type=F32)
            for a in range(3):
                re = product[16 * a : 16 * (a + 1)]
                im = product[48 + 16 * a : 48 + 16 * (a + 1)]
                mixed = pltpu.roll(jnp.where(lane, im, re), 64, 1)
                stage[pl.ds(512 * a + f, 16, stride=16), :] = jnp.where(lane, re, mixed)
                stage[pl.ds(512 * a + 256 + f, 16, stride=16), :] = jnp.where(lane, mixed, im)
        for a in range(3):
            send[b, :, :, a] = stage[pl.ds(512 * a, 512), :].reshape(2, 16, 16, 128).astype(BF16)

    def keep(b):
        target = stacks.at[b, slot] if b < 2 else last_ref.at[slot]
        return pltpu.make_async_copy(send.at[b, seg, slot // 2], target, own_sem.at[b])

    def ship(b, quarter):
        for px, py, pc in others[8 * quarter : 8 * quarter + 8]:
            pltpu.make_async_remote_copy(
                src_ref=send.at[b, py // 2, px * 4 + py % 2 * 2 + pc], dst_ref=stacks.at[b, slot] if b < 2 else last_ref.at[slot],
                send_sem=out_sem.at[b, 0], recv_sem=out_sem.at[b, 1],
                device_id=device(z, px, py, pc), device_id_type=MESH,
            ).start()
        if quarter == 3:
            keep(b).start()

    steps = {"F": forward, "A": arrive, "P": own_units, "L": own_side, "C": cross, "S": ship}
    for step in SCHEDULE:
        steps[step[0]](*(int(digit) for digit in step[1:]))

    loads[5].wait()
    for b in range(2):
        keep(b).wait()
        whole = stacks.at[b, pl.ds(0, 31)]
        pltpu.make_async_copy(whole, whole, out_sem.at[b, 1]).wait()
        rows = lag_rows([stacks[b, :, a].reshape(512, 128) for a in range(3)])
        for n in range(4):
            half = table_ref[2048 + 1024 * (n // 2) : 3072 + 1024 * (n // 2), 512 * (n % 2) : 512 * (n % 2 + 1)]
            lagged = jnp.dot(rows, half, preferred_element_type=F32)
            lags[b, :, :, pl.ds(512 * n, 512)] = lagged.astype(BF16).reshape(3, 64, 512)

    pltpu.make_async_copy(white.at[pl.ds(0, 31)], white.at[pl.ds(0, 31)], in_sem.at[0]).wait()
    for u in range(len(UNITS)):
        for reach in range(1, 5):
            for copy in moves(u, reach, 0):
                copy.wait_send()
    keep(2).wait()
    whole = last_ref.at[pl.ds(0, 31)]
    pltpu.make_async_copy(whole, whole, out_sem.at[2, 1]).wait()
    for b in range(3):
        pltpu.make_async_copy(whole, whole, out_sem.at[b, 0]).wait()


def in_hbm(array):
    return pltpu.with_memory_space_constraint(array, pltpu.HBM)


def stacked(records, availability, tables):
    vmem, hbm = pl.BlockSpec(memory_space=pltpu.VMEM), pl.BlockSpec(memory_space=pl.ANY)
    return pl.pallas_call(
        stack_kernel,
        name="stack",
        out_shape=(
            pltpu.VMEM((32, 3, 16, 128), BF16),
            pltpu.VMEM((2, 3, 64, 2 * LAG), BF16),
        ),
        in_specs=[hbm, hbm, hbm],
        out_specs=(vmem, vmem),
        scratch_shapes=[
            pltpu.VMEM((ROWS, 1, records.shape[2]), F32),
            pltpu.VMEM(availability.shape, jnp.int32),
            pltpu.VMEM(tables.shape, BF16),
            pltpu.VMEM((2, 32, 3, 16, 128), BF16),
            pltpu.VMEM((4, 256, 1024), BF16),
            pltpu.VMEM((32, 32, 128), F32),
            pltpu.VMEM((32, 32, 128), BF16),
            pltpu.VMEM((32, 32, 128), BF16),
            pltpu.VMEM((1024, 128), F32),
            pltpu.VMEM((3, 8, 16, 16, 128), BF16),
            pltpu.VMEM((16, 96, 128), BF16),
            pltpu.VMEM((1536, 128), F32),
            pltpu.VMEM((3, 2, 16, 3, 16, 128), BF16),
            pltpu.VMEM((2, 8, 128), F32),
            pltpu.SemaphoreType.DMA((6,)),
            pltpu.SemaphoreType.REGULAR,
            pltpu.SemaphoreType.REGULAR,
            pltpu.SemaphoreType.DMA((2,)),
            pltpu.SemaphoreType.DMA((2,)),
            pltpu.SemaphoreType.DMA((len(UNITS), 4, 2)),
            pltpu.SemaphoreType.DMA((len(UNITS), 4, 2)),
            pltpu.SemaphoreType.DMA((3, 2)),
            pltpu.SemaphoreType.DMA((3,)),
        ],
        compiler_params=pltpu.CompilerParams(
            collective_id=0, has_side_effects=True, vmem_limit_bytes=40 << 20
        ),
    )(in_hbm(records), in_hbm(availability), in_hbm(tables))


def lag_kernel(last_ref, part_ref, table_ref, out_hbm, lags, part_sem, out_sem):
    copies = [
        pltpu.make_async_copy(part_ref.at[b, a], out_hbm.at[3 * a + b], part_sem.at[b, a])
        for b in range(2)
        for a in range(3)
    ]
    for copy in copies:
        copy.start()
    rows = lag_rows([last_ref[:, a].reshape(512, 128) for a in range(3)])
    for n in range(4):
        column = pl.ds(512 * n, 512)
        lagged = jnp.dot(rows, table_ref[:, column], preferred_element_type=F32)
        lags[:, :, column] = lagged.astype(BF16).reshape(3, 64, 512)
        for a in range(3):
            copies.append(
                pltpu.make_async_copy(
                    lags.at[a, :, column], out_hbm.at[3 * a + 2, :, column], out_sem.at[n, a]
                )
            )
            copies[-1].start()
    for copy in copies:
        copy.wait()


def to_lags(last, part, table):
    vmem = pl.BlockSpec(memory_space=pltpu.VMEM)
    return pl.pallas_call(
        lag_kernel,
        name="lags",
        out_shape=jax.ShapeDtypeStruct((9, 64, 2 * LAG), BF16),
        in_specs=[vmem] * 3,
        out_specs=pl.BlockSpec(memory_space=pl.ANY),
        scratch_shapes=[
            pltpu.VMEM((3, 64, 2 * LAG), BF16),
            pltpu.SemaphoreType.DMA((2, 3)),
            pltpu.SemaphoreType.DMA((4, 3)),
        ],
        compiler_params=pltpu.CompilerParams(vmem_limit_bytes=40 << 20),
    )(*(pltpu.with_memory_space_constraint(array, pltpu.VMEM) for array in (last, part, table)))


def body(records, availability):
    samples = records.shape[-1]
    inverse = inverse_table()
    last, part = stacked(records.reshape(90, 1, samples), availability, jnp.asarray(all_tables(inverse)))
    lagged = to_lags(last, part, jnp.asarray(inverse))
    return jnp.transpose(lagged, (1, 0, 2))[None]


def solution(mesh):
    placed = (P("blk", "seg", None, None), P("blk", "seg"))
    return jax.shard_map(
        body, mesh=mesh, in_specs=placed, out_specs=P("blk", "seg", None, None), check_vma=False
    )
```

```python
import functools
import math

import jax
import jax.numpy as jnp
import ml_dtypes
import numpy as np
from jax import lax
from jax.experimental import pallas as pl
from jax.experimental.pallas import tpu as pltpu
from jax.sharding import PartitionSpec as P

MESH = pl.DeviceIdType.MESH
F32 = jnp.float32
BF16 = jnp.bfloat16
NFFT = 4096
FREQS = 512
LAG = 1024
SEGS = 30
ROWS = 96
RESIDUES = ((1, 7), (2, 6), (3, 5), (8, 4))
HALF = math.sqrt(0.5)
UNITS = ((0, 0, 8), (0, 8, 8), (1, 0, 16), (2, 0, 16))
OTHERS = sorted(
    ((dx, dy, dc) for dx in range(4) for dy in range(4) for dc in range(2) if dx or dy or dc),
    key=lambda d: (-min(d[0], 4 - d[0]) - min(d[1], 4 - d[1]), (5 * d[0] + 3 * d[1] + d[2]) % 7),
)
SCHEDULE = (
    ["P0", "F010", "P1", "F110", "F210", "A01", "F021", "A11", "F121", "F310", "L", "A21", "F221"]
    + ["A02", "F032", "F042", "A12", "F132", "F142", "A31", "F321", "A22", "F232", "F242"]
    + ["A03", "A13", "A04", "A14", "C0", "S00", "S01", "A32", "F332", "F342", "S02", "S03"]
    + ["A23", "A24", "C1", "S10", "S11", "S12", "S13"]
    + ["A33", "A34", "C2", "S20", "S21", "S22", "S23"]
)
NT = (((1,), (1,)), ((), ()))


def bin_of(p, f):
    return 16 * p + 8 * (f % 2) + np.array(RESIDUES)[f // 4, f // 2 % 2]


def forward_table():
    table = np.zeros((4, 32, 2, 2, 2, 2, 512))
    n = np.arange(512)
    for g in range(4):
        for which in range(2):
            for odd in range(2):
                k = 16 * np.arange(32) + 8 * odd + RESIDUES[g][which]
                angle = (k[:, None] * n[None, :] % NFFT) * (2 * np.pi / NFFT)
                cos, sin = np.cos(angle), np.sin(angle)
                if g == 3:
                    table[g, :, which, odd, 0, which] = cos
                    table[g, :, which, odd, 1, which] = -sin
                else:
                    sign = 1 - 2 * which
                    table[g, :, which, odd, 0, 0] = cos
                    table[g, :, which, odd, 0, 1] = sign * sin
                    table[g, :, which, odd, 1, 0] = -sin
                    table[g, :, which, odd, 1, 1] = sign * cos
    table = table.reshape(4, 256, 1024)
    high = table.astype(ml_dtypes.bfloat16)
    low = (table - high.astype(np.float64)).astype(ml_dtypes.bfloat16)
    return high.reshape(1024, 1024), low.reshape(1024, 1024)


def inverse_table():
    p, f = np.meshgrid(np.arange(32), np.arange(16), indexing="ij")
    k = bin_of(p, f).reshape(-1)
    tau = np.arange(2 * LAG) - LAG
    angle = (k[:, None] * tau[None, :] % NFFT) * (2 * np.pi / NFFT)
    table = np.concatenate([np.cos(angle), -np.sin(angle)], axis=0) * (2.0 / NFFT)
    return table.astype(ml_dtypes.bfloat16)


def place_table():
    plain = np.zeros((2, 2, 128, 4, 128))
    turned = np.zeros((2, 2, 128, 4, 128))
    for seg in range(2):
        for s in range(SEGS):
            for c in range(3):
                for part in range(2):
                    plain[seg, part, 3 * s + c, c, 64 * part + 30 * seg + s] = 1
                turned[seg, 1, 3 * s + c, c, 30 * seg + s] = 1
                turned[seg, 0, 3 * s + c, c, 64 + 30 * seg + s] = -1
    both = np.concatenate([plain.reshape(512, 512), turned.reshape(512, 512)], axis=1)
    return both.astype(ml_dtypes.bfloat16)


def all_tables(inverse):
    return np.concatenate([*forward_table(), inverse[:, :LAG], inverse[:, LAG:], place_table()], axis=0)


def place():
    blk, seg = lax.axis_index("blk"), lax.axis_index("seg")
    z, rest = blk // 16, blk % 16
    return z, rest // 4, seg * 2 + rest // 2 % 2, rest % 2, seg


def device(z, x, y, core):
    return (z * 16 + x * 4 + y % 2 * 2 + core, y // 2)


def lag_rows(blocks):
    turned = [block.T for block in blocks]
    return jnp.concatenate([jnp.concatenate([one[:64], one[64:]], axis=1) for one in turned], axis=0)


def spread(av):
    column = lax.broadcasted_iota(jnp.int32, (SEGS, 128), 1)
    row = lax.broadcasted_iota(jnp.int32, (SEGS, 128), 0)
    pick = ((column >= 3 * row) & (column < 3 * row + 3)).astype(F32)
    return jnp.dot(jnp.broadcast_to(av, (8, SEGS)), pick, preferred_element_type=F32)


def split_rows(w_ref, g, half, value):
    high = value.astype(BF16)
    low = (value - high.astype(F32)).astype(BF16)
    columns = pl.ds(512 * half, 512)
    w_ref[g, pl.ds(0, ROWS), columns] = high
    w_ref[g, pl.ds(128, ROWS), columns] = low


def stack_kernel(
    x_hbm, av_hbm, table_hbm, last_ref, lags,
    x_ref, av_ref, table_ref, stacks,
    w, xs, white, rin, turn, gathered, left, stage, send, counts,
    load_sem, line_sem, core_sem, count_sem, in_sem, ring_send, ring_recv, out_sem, own_sem,
):
    z, x, y, core, seg = place()
    slot = (x * 4 + y % 2 * 2 + core) * 2 + seg
    others = [((x + dx) % 4, (y + dy) % 4, (core + dc) % 2) for dx, dy, dc in OTHERS]
    parts = [pl.ds(first, rows) for first, rows in ((0, 1024), (1024, 1024), (4096, 512), (2048, 2048))]
    loads = [pltpu.make_async_copy(x_hbm, x_ref.at[pl.ds(0, 90)], load_sem.at[4]), pltpu.make_async_copy(av_hbm, av_ref, load_sem.at[5])]
    loads += [
        pltpu.make_async_copy(table_hbm.at[rows], table_ref.at[rows], load_sem.at[n]) for n, rows in enumerate(parts)
    ]
    for load in loads:
        load.start()

    barrier = pltpu.get_barrier_semaphore()

    lines = [((x + n) % 4, y, core) for n in range(1, 4)]
    near = [device(z, x, (y + n) % 4, core) for n in (2, 1, 3)]
    near += [device(z, *at) for at in lines]
    near += [device(z, x, y, 1 - core)]
    near += [device((z + n) % 8, x, y, core) for n in (1, 2, 6, 7)]
    for other in near:
        pl.semaphore_signal(barrier, inc=1, device_id=other, device_id_type=MESH)

    loads[1].wait()
    own = spread(av_ref[...].astype(F32))
    counts[0] = own
    for g in range(4):
        for start in (ROWS, 128 + ROWS):
            w[g, pl.ds(start, 32), :] = jnp.zeros((32, 1024), BF16)
    x_ref[pl.ds(90, ROWS - 90)] = jnp.zeros((ROWS - 90, 1, x_ref.shape[2]), F32)
    loads[0].wait()
    part = [x_ref[:, 0, pl.ds(512 * n, 512)] for n in range(5)]
    part.append(jnp.concatenate([x_ref[:, 0, pl.ds(2560, 440)], jnp.zeros((ROWS, 72), F32)], axis=1))
    d04 = part[0] - part[4]
    d13, s13 = part[1] - part[3], part[1] + part[3]
    split_rows(w, 0, 0, d04 + (d13 - part[5]) * HALF)
    split_rows(w, 0, 1, (part[5] - s13) * HALF - part[2])
    split_rows(w, 1, 0, part[0] + part[4] - part[2])
    split_rows(w, 1, 1, part[3] - part[1] - part[5])
    split_rows(w, 2, 0, d04 + (part[5] - d13) * HALF)
    split_rows(w, 2, 1, (part[5] - s13) * HALF + part[2])
    even, odd = part[0] + part[2] + part[4], s13 + part[5]
    split_rows(w, 3, 0, even + odd)
    split_rows(w, 3, 1, even - odd)

    pl.semaphore_wait(barrier, 11)
    count_copy = pltpu.make_async_remote_copy(
        src_ref=counts.at[0], dst_ref=counts.at[1], send_sem=count_sem.at[0], recv_sem=count_sem.at[1],
        device_id=device(z, x, (y + 2) % 4, core), device_id_type=MESH,
    )
    count_copy.start()
    for at in lines:
        pl.semaphore_signal(line_sem, inc=1, device_id=device(z, *at), device_id_type=MESH)

    power = jnp.zeros((32, 8, 128), F32)
    loads[2].wait()
    loads[3].wait()
    for g in range(4):
        if g == 2:
            pl.semaphore_wait(line_sem, 3)
            pl.semaphore_signal(core_sem, inc=1, device_id=device(z, x, y, 1 - core), device_id_type=MESH)
        high = lax.dot_general(table_ref[256 * g : 256 * (g + 1)], w[g], NT, preferred_element_type=F32)
        low = lax.dot_general(table_ref[1024 + 256 * g : 1280 + 256 * g], w[g], NT, preferred_element_type=F32)
        both = high + low
        value = (both[:, :128] + both[:, 128:]).reshape(32, 8, 128)
        xs[:, pl.ds(8 * g, 8), :] = value
        power = power + value * value
    power = jnp.sum(power.reshape(16, 16, 128), axis=1)
    triple = power + pltpu.roll(power, 127, 1) + pltpu.roll(power, 126, 1)
    phase = lax.broadcasted_iota(jnp.int32, (16, 128), 1) % 3
    total = jnp.where(phase == 0, triple, jnp.where(phase == 1, pltpu.roll(triple, 1, 1), pltpu.roll(triple, 2, 1)))
    amplitude = jnp.sqrt(total * (1.0 / 96) + 1e-06)
    factor = own[0:1] / amplitude
    xs[...] = (xs[...].reshape(16, 64, 128) * factor[:, None, :]).reshape(32, 32, 128)
    count_copy.wait()
    count = (jnp.sum(own, axis=1, keepdims=True) + jnp.sum(counts[1], axis=1, keepdims=True)) * (1.0 / 3)
    scale = jnp.broadcast_to(1.0 / jnp.sqrt(jnp.round(count)), (8, 128))[0:1]
    white[...] = (xs[...] * scale[None]).astype(BF16)

    pl.semaphore_wait(core_sem, 1)

    for px, py, pc in others:
        target = (px * 4 + py % 2 * 2 + pc) * 2 + py // 2
        pltpu.make_async_remote_copy(
            src_ref=white.at[target], dst_ref=rin.at[slot], send_sem=in_sem.at[0], recv_sem=in_sem.at[1],
            device_id=device(z, px, py, pc), device_id_type=MESH,
        ).start()
    pltpu.make_async_copy(rin.at[pl.ds(0, 31)], rin.at[pl.ds(0, 31)], in_sem.at[1]).wait()
    rin[slot] = white[slot]

    def swap(source, carry):
        start = source % 2 * 512 + source // 2
        turn[pl.ds(start, 32, stride=16), :] = rin[source].astype(F32)
        return carry

    lax.fori_loop(0, 32, swap, 0)
    loads[4].wait()
    pieces = turn[...].reshape(2, 16, 2, 16, 128)
    rows = jnp.concatenate(
        [pieces[s, :, part].reshape(256, 128).astype(BF16) for s in range(2) for part in range(2)], axis=1
    )
    def own_units(half):
        plain = jnp.dot(rows[128 * half : 128 * half + 128], table_ref[4096:, :384], preferred_element_type=F32)
        plain = plain.astype(BF16)
        for c in range(3):
            gathered[c, z, pl.ds(8 * half, 8)] = plain[:, 128 * c : 128 * (c + 1)].reshape(8, 16, 128)

    def moves(u, reach, come):
        c, first, bins = UNITS[u]
        signs = (1, -1) if reach < 4 else (1 - 2 * core,)
        for way, sign in enumerate(signs):
            piece = gathered.at[c, (z + 8 - sign * come) % 8, pl.ds(first, bins)]
            yield pltpu.make_async_remote_copy(
                src_ref=piece, dst_ref=piece,
                send_sem=ring_send.at[u, reach - 1, way], recv_sem=ring_recv.at[u, reach - 1, way],
                device_id=device((z + 8 + sign * (reach - come)) % 8, x, y, core), device_id_type=MESH,
            )

    def forward(u, reach, come):
        for copy in moves(u, reach, come):
            copy.start()

    def arrive(u, reach):
        for copy in moves(u, reach, 0):
            copy.wait_recv()

    def own_side():
        turned = jnp.dot(rows, table_ref[4096:, 512:896], preferred_element_type=F32).astype(BF16)
        for c in range(3):
            left[:, pl.ds(16 * c, 16), :] = gathered[c, z]
            left[:, pl.ds(48 + 16 * c, 16), :] = turned[:, 128 * c : 128 * (c + 1)].reshape(16, 16, 128)

    lane = lax.broadcasted_iota(jnp.int32, (16, 128), 1) < 64

    def cross(b):
        for f in range(16):
            right = gathered[b, :, f].reshape(128, 128)
            product = lax.dot_general(left[f], right, NT, preferred_element_type=F32)
            for a in range(3):
                re = product[16 * a : 16 * (a + 1)]
                im = product[48 + 16 * a : 48 + 16 * (a + 1)]
                mixed = pltpu.roll(jnp.where(lane, im, re), 64, 1)
                stage[pl.ds(512 * a + f, 16, stride=16), :] = jnp.where(lane, re, mixed)
                stage[pl.ds(512 * a + 256 + f, 16, stride=16), :] = jnp.where(lane, mixed, im)
        for a in range(3):
            send[b, :, :, a] = stage[pl.ds(512 * a, 512), :].reshape(2, 16, 16, 128).astype(BF16)

    def keep(b):
        target = stacks.at[b, slot] if b < 2 else last_ref.at[slot]
        return pltpu.make_async_copy(send.at[b, seg, slot // 2], target, own_sem.at[b])

    def ship(b, quarter):
        for px, py, pc in others[8 * quarter : 8 * quarter + 8]:
            pltpu.make_async_remote_copy(
                src_ref=send.at[b, py // 2, px * 4 + py % 2 * 2 + pc], dst_ref=stacks.at[b, slot] if b < 2 else last_ref.at[slot],
                send_sem=out_sem.at[b, 0], recv_sem=out_sem.at[b, 1],
                device_id=device(z, px, py, pc), device_id_type=MESH,
            ).start()
        if quarter == 3:
            keep(b).start()

    steps = {"F": forward, "A": arrive, "P": own_units, "L": own_side, "C": cross, "S": ship}
    for step in SCHEDULE:
        steps[step[0]](*(int(digit) for digit in step[1:]))

    loads[5].wait()
    for b in range(2):
        keep(b).wait()
        whole = stacks.at[b, pl.ds(0, 31)]
        pltpu.make_async_copy(whole, whole, out_sem.at[b, 1]).wait()
        rows = lag_rows([stacks[b, :, a].reshape(512, 128) for a in range(3)])
        for n in range(4):
            half = table_ref[2048 + 1024 * (n // 2) : 3072 + 1024 * (n // 2), 512 * (n % 2) : 512 * (n % 2 + 1)]
            lagged = jnp.dot(rows, half, preferred_element_type=F32)
            lags[b, :, :, pl.ds(512 * n, 512)] = lagged.astype(BF16).reshape(3, 64, 512)

    pltpu.make_async_copy(white.at[pl.ds(0, 31)], white.at[pl.ds(0, 31)], in_sem.at[0]).wait()
    for u in range(len(UNITS)):
        for reach in range(1, 5):
            for copy in moves(u, reach, 0):
                copy.wait_send()
    keep(2).wait()
    whole = last_ref.at[pl.ds(0, 31)]
    pltpu.make_async_copy(whole, whole, out_sem.at[2, 1]).wait()
    for b in range(3):
        pltpu.make_async_copy(whole, whole, out_sem.at[b, 0]).wait()


def in_hbm(array):
    return pltpu.with_memory_space_constraint(array, pltpu.HBM)


def stacked(records, availability, tables):
    vmem, hbm = pl.BlockSpec(memory_space=pltpu.VMEM), pl.BlockSpec(memory_space=pl.ANY)
    return pl.pallas_call(
        stack_kernel,
        name="stack",
        out_shape=(
            pltpu.VMEM((32, 3, 16, 128), BF16),
            pltpu.VMEM((2, 3, 64, 2 * LAG), BF16),
        ),
        in_specs=[hbm, hbm, hbm],
        out_specs=(vmem, vmem),
        scratch_shapes=[
            pltpu.VMEM((ROWS, 1, records.shape[2]), F32),
            pltpu.VMEM(availability.shape, jnp.int32),
            pltpu.VMEM(tables.shape, BF16),
            pltpu.VMEM((2, 32, 3, 16, 128), BF16),
            pltpu.VMEM((4, 256, 1024), BF16),
            pltpu.VMEM((32, 32, 128), F32),
            pltpu.VMEM((32, 32, 128), BF16),
            pltpu.VMEM((32, 32, 128), BF16),
            pltpu.VMEM((1024, 128), F32),
            pltpu.VMEM((3, 8, 16, 16, 128), BF16),
            pltpu.VMEM((16, 96, 128), BF16),
            pltpu.VMEM((1536, 128), F32),
            pltpu.VMEM((3, 2, 16, 3, 16, 128), BF16),
            pltpu.VMEM((2, 8, 128), F32),
            pltpu.SemaphoreType.DMA((6,)),
            pltpu.SemaphoreType.REGULAR,
            pltpu.SemaphoreType.REGULAR,
            pltpu.SemaphoreType.DMA((2,)),
            pltpu.SemaphoreType.DMA((2,)),
            pltpu.SemaphoreType.DMA((len(UNITS), 4, 2)),
            pltpu.SemaphoreType.DMA((len(UNITS), 4, 2)),
            pltpu.SemaphoreType.DMA((3, 2)),
            pltpu.SemaphoreType.DMA((3,)),
        ],
        compiler_params=pltpu.CompilerParams(
            collective_id=0, has_side_effects=True, vmem_limit_bytes=40 << 20
        ),
    )(in_hbm(records), in_hbm(availability), in_hbm(tables))


def lag_kernel(last_ref, part_ref, table_ref, out_hbm, lags, part_sem, out_sem):
    copies = [
        pltpu.make_async_copy(part_ref.at[b, a], out_hbm.at[3 * a + b], part_sem.at[b, a])
        for b in range(2)
        for a in range(3)
    ]
    for copy in copies:
        copy.start()
    rows = lag_rows([last_ref[:, a].reshape(512, 128) for a in range(3)])
    for n in range(4):
        column = pl.ds(512 * n, 512)
        lagged = jnp.dot(rows, table_ref[:, column], preferred_element_type=F32)
        lags[:, :, column] = lagged.astype(BF16).reshape(3, 64, 512)
        for a in range(3):
            copies.append(
                pltpu.make_async_copy(
                    lags.at[a, :, column], out_hbm.at[3 * a + 2, :, column], out_sem.at[n, a]
                )
            )
            copies[-1].start()
    for copy in copies:
        copy.wait()


def to_lags(last, part, table):
    vmem = pl.BlockSpec(memory_space=pltpu.VMEM)
    return pl.pallas_call(
        lag_kernel,
        name="lags",
        out_shape=jax.ShapeDtypeStruct((9, 64, 2 * LAG), BF16),
        in_specs=[vmem] * 3,
        out_specs=pl.BlockSpec(memory_space=pl.ANY),
        scratch_shapes=[
            pltpu.VMEM((3, 64, 2 * LAG), BF16),
            pltpu.SemaphoreType.DMA((2, 3)),
            pltpu.SemaphoreType.DMA((4, 3)),
        ],
        compiler_params=pltpu.CompilerParams(vmem_limit_bytes=40 << 20),
    )(*(pltpu.with_memory_space_constraint(array, pltpu.VMEM) for array in (last, part, table)))


def body(records, availability):
    samples = records.shape[-1]
    inverse = inverse_table()
    last, part = stacked(records.reshape(90, 1, samples), availability, jnp.asarray(all_tables(inverse)))
    lagged = to_lags(last, part, jnp.asarray(inverse))
    return jnp.transpose(lagged, (1, 0, 2))[None]


def solution(mesh):
    placed = (P("blk", "seg", None, None), P("blk", "seg"))
    return jax.shard_map(
        body, mesh=mesh, in_specs=placed, out_specs=P("blk", "seg", None, None), check_vma=False
    )
```
